32 devices in a mesh: bin: 16 (over z, y, x), grp: 2 (over core).
Axes of the slice: x: 2, y: 2, z: 4, core: 2. Of those that a mesh axis runs over, the one named last changes fastest.
Arguments:
- record: bfloat16 [2, 1024, 8704], P('grp', 'bin'), may hold values from -60 to 60
- ref_index: int32 [2, 64], P('grp'), may hold values from 0 to 1023, as said below
- offsets: int32 [16], replicated, may hold values from 0 to 7680, as said below
Outputs:
- transfer: bfloat16 [512, 2048, 256], P('bin', 'grp')
The draws below stay inside these ranges and needn't reach their ends.
Inputs may be any that keep to these rules, and one draw needn't show every extreme that they name: `ref_index`: each row lists 64 different channels of its group; every row holds 0 and 1023. `offsets`: starts rise; the first is 0, the last is 7680, and neighbours lie 512 // 2 to 768 apart.
All inputs are finite; a program needn't handle non-finite values.
Results may differ from the reference program's by a relative error of at most 0.0095.
Values may be sent and summed in bfloat16 or wider, within the bound.
No kernel may reach another device: no remote copies, remote signals or barrier semaphores. Data moves between devices by JAX's collectives and lax.ppermute only.
A program may use at most 64 MiB of HBM per device.

```python
import math
import jax
import jax.numpy as jnp
from jax import lax

C = 2048
R = 128
L = 1024
NB = 512
SEGS = 16
HOP = 512
NSAMP = 8704
GRP_COUNT = 2
CH_GRP = 1024
REF_GRP = 64


def draw_record(key, part):
    key_noise, key_scale = jax.random.split(key, 2)
    shape_full = (GRP_COUNT, CH_GRP, NSAMP)
    chan_scale = jnp.exp(jax.random.uniform(key_scale, (GRP_COUNT, CH_GRP, 1), jnp.float32, 0.0, math.log(10.0)))
    noise = jnp.clip(jax.random.normal(key_noise, shape_full, jnp.float32), -6.0, 6.0)
    values = noise * chan_scale
    return values.astype(jnp.bfloat16)


def draw_ref_index(key, part):

    def one_group(group_key):
        key_pick, key_order = jax.random.split(group_key)
        middle = jax.random.permutation(key_pick, CH_GRP - 2)[:REF_GRP - 2].astype(jnp.int32) + 1
        chosen = jnp.concatenate([jnp.array([0, CH_GRP - 1], dtype=jnp.int32), middle])
        return jax.random.permutation(key_order, chosen)
    return jax.vmap(one_group)(jax.random.split(key, GRP_COUNT)).astype(jnp.int32)


def draw_offsets(key, part):
    jitter = jax.random.randint(key, (SEGS,), -(HOP // 4), HOP // 4 + 1, dtype=jnp.int32)
    segment_num = jnp.arange(SEGS, dtype=jnp.int32)
    inner = (segment_num > 0) & (segment_num < SEGS - 1)
    return (segment_num * HOP + jnp.where(inner, jitter, 0)).astype(jnp.int32)


def setup_inputs(seed: int = 0) -> dict:
    streams_of = jax.random.split(jax.random.key(seed), 4)
    return {
        "record": draw_record(jax.random.fold_in(streams_of[3], 71), 0),
        "ref_index": draw_ref_index(jax.random.fold_in(streams_of[3], 71), 0),
        "offsets": draw_offsets(jax.random.fold_in(streams_of[3], 71), 0),
    }


ridge_weight = 0.5

def make_table(seg_len, bins):
    sample_num = lax.iota(jnp.int32, seg_len)[:, None]
    bin_num = lax.iota(jnp.int32, bins)[None, :]
    angles = (sample_num * bin_num % seg_len).astype(jnp.float32) * (2.0 * math.pi / seg_len)
    hann_window = 0.5 - 0.5 * jnp.cos(sample_num.astype(jnp.float32) * (2.0 * math.pi / seg_len))
    return jnp.concatenate([hann_window * jnp.cos(angles), -(hann_window * jnp.sin(angles))], axis=1).astype(jnp.bfloat16)

def reference(record, ref_index, offsets):
    chan_rows = record.reshape(C, NSAMP)
    dft_table = make_table(L, NB).astype(jnp.float32)

    def one_segment(start_at):
        piece = lax.dynamic_slice_in_dim(chan_rows, start_at, L, 1).astype(jnp.float32)
        return jnp.dot(piece.astype(jnp.float32), dft_table.astype(jnp.float32), precision=lax.Precision.HIGHEST, preferred_element_type=jnp.float32).astype(jnp.bfloat16)
    spectra = lax.map(one_segment, offsets)
    spectra = jnp.transpose(spectra.reshape(SEGS, C, 2, NB), (3, 2, 0, 1))
    ref_channel = (ref_index + jnp.arange(GRP_COUNT, dtype=jnp.int32)[:, None] * CH_GRP).reshape(R).astype(jnp.int32)

    def one_bin(chan_spec):
        refs = jnp.take(chan_spec, ref_channel, axis=2).astype(jnp.float32)
        ref_real = refs[0]
        ref_imag = refs[1]
        ref_blocks = jnp.stack([jnp.concatenate([ref_real, -ref_imag], axis=-1), jnp.concatenate([ref_imag, ref_real], axis=-1)]).reshape(2 * SEGS, 2 * R)
        gram_small = jnp.dot(ref_blocks.astype(jnp.float32), ref_blocks.T.astype(jnp.float32), precision=lax.Precision.HIGHEST, preferred_element_type=jnp.float32)
        ridge_term = ridge_weight * jnp.trace(gram_small) / (2 * R)
        factor = jnp.linalg.cholesky(gram_small + ridge_term * jnp.eye(2 * SEGS, dtype=jnp.float32))
        chan_cols = chan_spec.reshape(2 * SEGS, C).astype(jnp.float32)
        solved = jax.scipy.linalg.cho_solve((factor, True), chan_cols)
        transfer_t = jnp.dot(ref_blocks.T.astype(jnp.float32), solved.astype(jnp.float32), precision=lax.Precision.HIGHEST, preferred_element_type=jnp.float32)
        return transfer_t.T.astype(jnp.bfloat16)
    return lax.map(one_bin, spectra)
```

```python
import math

import jax
import jax.numpy as jnp
import numpy as np
from jax import lax
from jax.experimental import pallas as pl
from jax.experimental.pallas import tpu as pltpu
from jax.sharding import PartitionSpec as P

L = 1024
NB = 512
LANES = 128
SUB = 8
VMEM_LIMIT = 48 * 1024 * 1024
CHUNKS = (3, 1)

ridge_weight = 0.5


def make_table(seg_len, bins):
    sample_num = lax.iota(jnp.int32, seg_len)[:, None]
    bin_num = lax.iota(jnp.int32, bins)[None, :]
    angles = (sample_num * bin_num % seg_len).astype(jnp.float32) * (2.0 * math.pi / seg_len)
    hann_window = 0.5 - 0.5 * jnp.cos(sample_num.astype(jnp.float32) * (2.0 * math.pi / seg_len))
    return jnp.concatenate(
        [hann_window * jnp.cos(angles), -(hann_window * jnp.sin(angles))], axis=1
    ).astype(jnp.bfloat16)


def host_table(seg_len, bins):
    step = np.float32(2.0 * math.pi / seg_len)
    sample_num = np.arange(seg_len, dtype=np.int64)
    bin_num = np.arange(bins, dtype=np.int64)[:, None]
    angles = (sample_num[None, :] * bin_num % seg_len).astype(np.float32) * step
    hann_window = np.float32(0.5) - np.float32(0.5) * np.cos(sample_num.astype(np.float32) * step)
    return np.stack([hann_window * np.cos(angles), -(hann_window * np.sin(angles))]).astype(jnp.bfloat16)


def spectra_kernel(starts_ref, record_ref, table_ref, out_ref, pieces_ref):
    chans, samples = record_ref.shape
    seg_len = table_ref.shape[1]
    segs = starts_ref.shape[0]
    wide = seg_len + LANES
    per_dot = max(1, 256 // chans)
    for first in range(0, segs, per_dot):
        for seg in range(first, first + per_dot):
            start = starts_ref[seg]
            base = jnp.minimum(start // LANES * LANES, samples - wide)
            window = record_ref[:, pl.ds(pl.multiple_of(base, LANES), wide)].astype(jnp.float32)
            shift = lax.rem(wide - (start - base), wide)
            piece = pltpu.roll(window, shift, 1)[:, :seg_len]
            pieces_ref[pl.ds(seg * chans, chans), :] = piece.astype(jnp.bfloat16)
        cols = pl.ds(first * chans, per_dot * chans)
        out_ref[:, cols] = lax.dot_general(
            table_ref[...],
            pieces_ref[cols, :],
            (((1,), (1,)), ((), ())),
            preferred_element_type=jnp.float32,
        ).astype(jnp.bfloat16)


def spectra_of(record, offsets, table):
    chans = record.shape[0]
    segs = offsets.shape[0]
    rows, seg_len = table.shape
    cols = segs * chans
    return pl.pallas_call(
        spectra_kernel,
        out_shape=jax.ShapeDtypeStruct((rows, cols), jnp.bfloat16),
        in_specs=[
            pl.BlockSpec(memory_space=pltpu.SMEM),
            pl.BlockSpec(memory_space=pltpu.VMEM),
            pl.BlockSpec(memory_space=pltpu.VMEM),
        ],
        out_specs=pl.BlockSpec(memory_space=pltpu.VMEM),
        scratch_shapes=[pltpu.VMEM((cols, seg_len), jnp.bfloat16)],
        compiler_params=pltpu.CompilerParams(vmem_limit_bytes=VMEM_LIMIT),
        cost_estimate=pl.CostEstimate(
            flops=2 * rows * cols * seg_len, bytes_accessed=4 * rows * cols, transcendentals=0
        ),
        name="spectra",
    )(offsets, record, table)


def pick_kernel(index_ref, got_ref, out_ref):
    sources, rows, _ = got_ref.shape
    chans = LANES // 2
    group_rows = 2 * SUB
    tiles = got_ref.shape[2] // LANES
    index = index_ref[...]
    chan = lax.broadcasted_iota(jnp.int32, (LANES, LANES), 0)
    col = lax.broadcasted_iota(jnp.int32, (LANES, LANES), 1)
    same_seg = (chan >= chans) == (col >= chans)
    chan = jnp.where(chan >= chans, chan - chans, chan)
    picks = []
    for source in range(sources):
        hit = same_seg & (chan + source * chans == index)
        picks.append(jnp.where(hit, 1.0, 0.0).astype(jnp.bfloat16))
    for group in range(rows // group_rows):
        total = jnp.zeros((tiles * group_rows, LANES), jnp.float32)
        for source in range(sources):
            block = jnp.concatenate(
                [
                    got_ref[source, pl.ds(group * group_rows, group_rows), pl.ds(tile * LANES, LANES)]
                    for tile in range(tiles)
                ],
                axis=0,
            )
            total = total + jnp.dot(block, picks[source], preferred_element_type=jnp.float32)
        out_ref[group] = total.astype(jnp.bfloat16)


def pick_refs(index, got):
    sources, rows, cols = got.shape
    groups = rows // (2 * SUB)
    out_rows = cols // LANES * 2 * SUB
    return pl.pallas_call(
        pick_kernel,
        out_shape=jax.ShapeDtypeStruct((groups, out_rows, LANES), jnp.bfloat16),
        in_specs=[pl.BlockSpec(memory_space=pltpu.VMEM)] * 2,
        out_specs=pl.BlockSpec(memory_space=pltpu.VMEM),
        compiler_params=pltpu.CompilerParams(vmem_limit_bytes=VMEM_LIMIT),
        cost_estimate=pl.CostEstimate(
            flops=2 * groups * out_rows * sources * LANES * LANES,
            bytes_accessed=2 * sources * rows * cols,
            transcendentals=0,
        ),
        name="pick_refs",
    )(index, got)


def turn_kernel(got_ref, out_ref):
    sources, rows, _ = got_ref.shape
    chans = LANES // 2
    group_rows = 2 * SUB
    tiles = got_ref.shape[2] // LANES
    for group in range(rows // group_rows):
        for source in range(sources):
            block = jnp.concatenate(
                [
                    got_ref[source, pl.ds(group * group_rows, group_rows), pl.ds(tile * LANES, LANES)]
                    for tile in range(tiles)
                ],
                axis=0,
            )
            turned = block.T
            here = pl.ds(source * chans, chans)
            out_ref[group, here, 0:LANES] = turned[:chans]
            out_ref[group, here, LANES : 2 * LANES] = turned[chans:]


def turn(got):
    sources, rows, cols = got.shape
    groups = rows // (2 * SUB)
    return pl.pallas_call(
        turn_kernel,
        out_shape=jax.ShapeDtypeStruct((groups, sources * LANES // 2, 2 * LANES), jnp.bfloat16),
        in_specs=[pl.BlockSpec(memory_space=pltpu.VMEM)],
        out_specs=pl.BlockSpec(memory_space=pltpu.VMEM),
        compiler_params=pltpu.CompilerParams(vmem_limit_bytes=VMEM_LIMIT),
        cost_estimate=pl.CostEstimate(
            flops=0, bytes_accessed=4 * sources * rows * cols, transcendentals=0
        ),
        name="turn",
    )(got)


def solve_group(refs, segs, total_refs):
    gram = {}
    for i in range(segs):
        for j in range(i + 1):
            (ir, ii), (jr, ji) = refs[i], refs[j]
            real = jnp.sum(ir * jr + ii * ji, axis=1, keepdims=True)
            imag = None if i == j else jnp.sum(ir * ji - ii * jr, axis=1, keepdims=True)
            gram[i, j] = (real, imag)
    trace = gram[0, 0][0]
    for i in range(1, segs):
        trace = trace + gram[i, i][0]
    ridge = ridge_weight * trace / total_refs
    wide = refs[0][0].shape
    spread = lambda x: jnp.broadcast_to(x, wide)
    real = {k: spread(v[0] + ridge if k[0] == k[1] else v[0]) for k, v in gram.items()}
    imag = {k: spread(v[1]) for k, v in gram.items() if k[0] != k[1]}
    right = [(r, -i) for r, i in refs]
    lower = {}
    inverse = []
    for k in range(segs):
        inv = 1.0 / real[k, k]
        inverse.append(inv)
        for i in range(k + 1, segs):
            lower[i, k] = (real[i, k] * inv, imag[i, k] * inv)
        for i in range(k + 1, segs):
            lr, li = lower[i, k]
            for j in range(k + 1, i):
                gr, gi = real[j, k], imag[j, k]
                real[i, j] = real[i, j] - (lr * gr + li * gi)
                imag[i, j] = imag[i, j] - (li * gr - lr * gi)
            real[i, i] = real[i, i] - (lr * real[i, k] + li * imag[i, k])
            br, bi = right[k]
            cr, ci = right[i]
            right[i] = (cr - (lr * br - li * bi), ci - (lr * bi + li * br))
    found = [None] * segs
    for k in range(segs - 1, -1, -1):
        br, bi = right[k]
        vr, vi = br * inverse[k], bi * inverse[k]
        for i in range(k + 1, segs):
            lr, li = lower[i, k]
            wr, wi = found[i]
            vr = vr - (lr * wr + li * wi)
            vi = vi - (lr * wi - li * wr)
        found[k] = (vr, vi)
    return found


def solve_kernel(refs_ref, turned_ref, *rest):
    out_ref, wide_ref = rest[-2], rest[-1]
    half = LANES // 2
    rows = refs_ref.shape[2]
    segs = 2 * rows // (2 * SUB)
    step = pl.program_id(1)

    @pl.when(step == 0)
    def _():
        low = refs_ref[0, 0].astype(jnp.float32)
        high = refs_ref[1, 0].astype(jnp.float32)
        left = lax.broadcasted_iota(jnp.int32, low.shape, 1) < half
        even = jnp.where(left, low, pltpu.roll(high, half, 1))
        odd = jnp.where(left, pltpu.roll(low, half, 1), high)
        refs = []
        for seg in range(segs):
            source = odd if seg % 2 else even
            at = seg // 2 * 2 * SUB
            refs.append((source[at : at + SUB], source[at + SUB : at + 2 * SUB]))
        found = solve_group(refs, segs, LANES)
        for seg in range(segs):
            vr, vi = found[seg]
            at = (seg % 2) * LANES + seg // 2 * 2 * SUB
            wide_ref[at : at + SUB, 0:LANES] = vr
            wide_ref[at : at + SUB, LANES : 2 * LANES] = vi
            wide_ref[at + SUB : at + 2 * SUB, 0:LANES] = -vi
            wide_ref[at + SUB : at + 2 * SUB, LANES : 2 * LANES] = vr

    row_bin = lax.broadcasted_iota(jnp.int32, wide_ref.shape, 0) % SUB
    weights = jnp.where(row_bin == step, wide_ref[...], 0.0).astype(jnp.bfloat16)
    out_ref[0] = jnp.dot(turned_ref[0], weights, preferred_element_type=jnp.float32).astype(
        jnp.bfloat16
    )


def solve_and_apply(refs, turned, bins, first_bin, before):
    groups, chans, depth = turned.shape
    first_group = first_bin // SUB
    operands = [refs, turned]
    specs = [
        pl.BlockSpec((2, 1, refs.shape[2], LANES), lambda g, f: (0, g, 0, 0)),
        pl.BlockSpec((1, chans, depth), lambda g, f: (g, 0, 0)),
    ]
    aliases = {}
    if before is not None:
        operands.append(before)
        specs.append(pl.BlockSpec(memory_space=pl.ANY))
        aliases = {2: 0}
    return pl.pallas_call(
        solve_kernel,
        grid=(groups, SUB),
        out_shape=jax.ShapeDtypeStruct((bins, chans, 2 * LANES), jnp.bfloat16),
        in_specs=specs,
        out_specs=pl.BlockSpec(
            (1, chans, 2 * LANES), lambda g, f: ((first_group + g) * SUB + f, 0, 0)
        ),
        scratch_shapes=[pltpu.VMEM((depth, 2 * LANES), jnp.float32)],
        input_output_aliases=aliases,
        compiler_params=pltpu.CompilerParams(
            vmem_limit_bytes=VMEM_LIMIT, dimension_semantics=("arbitrary", "arbitrary")
        ),
        cost_estimate=pl.CostEstimate(
            flops=2 * groups * SUB * chans * depth * 2 * LANES,
            bytes_accessed=groups * SUB * chans * 4 * LANES,
            transcendentals=0,
        ),
        name="solve_apply",
    )(*operands)


def local_kernels(record, ref_index, offsets):
    chan_rows = record[0]
    devices = lax.axis_size("bin")
    bins = NB // devices
    table = host_table(L, NB).reshape(2, devices, bins // SUB, SUB, L).transpose(1, 2, 0, 3, 4)
    index = jnp.concatenate([ref_index, ref_index], axis=1)
    out = None
    first_group = 0
    for groups in CHUNKS:
        part = table[:, first_group : first_group + groups].reshape(-1, L)
        sent = spectra_of(chan_rows, offsets, jnp.asarray(part))
        sent = sent.reshape(devices, groups * 2 * SUB, -1)
        got = lax.all_to_all(sent, "bin", 0, 0, tiled=True)
        own = pick_refs(index, got)
        refs = lax.all_gather(own, "grp", axis=0)
        turned = turn(got)
        out = solve_and_apply(refs, turned, bins, first_group * SUB, out)
        first_group += groups
    return out


def transform(chan_rows, starts, dft_table, bin_devices):
    seg_len = dft_table.shape[0]
    pieces = jax.vmap(lambda start_at: lax.dynamic_slice_in_dim(chan_rows, start_at, seg_len, 1))(
        starts
    )
    spectra = jnp.einsum(
        "scn,nk->ksc", pieces, dft_table, preferred_element_type=jnp.float32
    ).astype(jnp.bfloat16)
    bin_total = dft_table.shape[1] // 2
    return spectra.reshape(
        2, bin_devices, bin_total // bin_devices, starts.shape[0], chan_rows.shape[0]
    )


def local(record, ref_index, offsets):
    chan_rows = record[0]
    dft_table = make_table(L, NB)
    bin_devices = lax.axis_size("bin")
    spectra = transform(chan_rows, offsets, dft_table, bin_devices)
    channels = lax.all_to_all(spectra, "bin", split_axis=1, concat_axis=4, tiled=True)[:, 0]
    local_refs = jnp.take(channels, ref_index[0], axis=3)
    references = lax.all_gather(local_refs, "grp", axis=3, tiled=True)
    ref_real = references[0]
    ref_imag = references[1]
    ref_blocks = jnp.stack(
        [
            jnp.concatenate([ref_real, -ref_imag], axis=-1),
            jnp.concatenate([ref_imag, ref_real], axis=-1),
        ]
    )
    bins_here = channels.shape[1]
    group_size = math.gcd(bins_here, 4)
    group_count = bins_here // group_size
    real_order = ref_blocks.shape[-1]

    def solve_bins(group_index):
        first_bin = group_index * group_size
        ref_group = lax.dynamic_slice_in_dim(ref_blocks, first_bin, group_size, 1)
        chan_group = lax.dynamic_slice_in_dim(channels, first_bin, group_size, 1)
        ref_rows = jnp.swapaxes(ref_group, 0, 1).reshape(group_size, -1, real_order)
        chan_cols = jnp.swapaxes(chan_group, 0, 1).reshape(group_size, -1, chan_group.shape[-1])
        gram_small = jnp.einsum(
            "fkr,fjr->fkj", ref_rows, ref_rows, preferred_element_type=jnp.float32
        )
        small_order = gram_small.shape[-1]
        ridge_term = ridge_weight * jnp.trace(gram_small, axis1=1, axis2=2) / real_order
        factor = jnp.linalg.cholesky(
            gram_small + ridge_term[:, None, None] * jnp.eye(small_order, dtype=jnp.float32)
        )
        solved = jax.scipy.linalg.cho_solve((factor, True), chan_cols.astype(jnp.float32))
        solved_high = solved.astype(jnp.bfloat16)
        solved_low = (solved - solved_high.astype(jnp.float32)).astype(jnp.bfloat16)
        transfer_t = jnp.einsum(
            "fkr,fkc->frc", ref_rows, solved_high, preferred_element_type=jnp.float32
        )
        transfer_t = transfer_t + jnp.einsum(
            "fkr,fkc->frc", ref_rows, solved_low, preferred_element_type=jnp.float32
        )
        return jnp.swapaxes(transfer_t, 1, 2).astype(jnp.bfloat16)

    results = lax.map(solve_bins, jnp.arange(group_count))
    return results.reshape(bins_here, results.shape[2], results.shape[3])


def solution(mesh):
    placed = (P("grp", "bin", None), P("grp", None), P())
    devices, groups = mesh.shape["bin"], mesh.shape["grp"]

    def whole(record, ref_index, offsets):
        chans = record.shape[1] // devices
        kernels = (
            groups == 2
            and 2 * chans == LANES
            and groups * ref_index.shape[1] == LANES
            and offsets.shape[0] == 2 * SUB
            and NB // devices == sum(CHUNKS) * SUB
        )
        return jax.shard_map(
            local_kernels if kernels else local,
            mesh=mesh,
            in_specs=placed,
            out_specs=P("bin", "grp", None),
            check_vma=False,
        )(record, ref_index, offsets)

    return whole
```

```python
import math

import jax
import jax.numpy as jnp
import numpy as np
from jax import lax
from jax.experimental import pallas as pl
from jax.experimental.pallas import tpu as pltpu
from jax.sharding import PartitionSpec as P

L = 1024
NB = 512
LANES = 128
SUB = 8
VMEM_LIMIT = 48 * 1024 * 1024
SPECTRA_LIMIT = 66000000
MAX_GAP = 768

ridge_weight = 0.5


def make_table(seg_len, bins):
    sample_num = lax.iota(jnp.int32, seg_len)[:, None]
    bin_num = lax.iota(jnp.int32, bins)[None, :]
    angles = (sample_num * bin_num % seg_len).astype(jnp.float32) * (2.0 * math.pi / seg_len)
    hann_window = 0.5 - 0.5 * jnp.cos(sample_num.astype(jnp.float32) * (2.0 * math.pi / seg_len))
    return jnp.concatenate(
        [hann_window * jnp.cos(angles), -(hann_window * jnp.sin(angles))], axis=1
    ).astype(jnp.bfloat16)


def host_table(seg_len, bins):
    step = np.float32(2.0 * math.pi / seg_len)
    sample_num = np.arange(seg_len, dtype=np.int64)
    bin_num = np.arange(bins, dtype=np.int64)[:, None]
    angles = (sample_num[None, :] * bin_num % seg_len).astype(np.float32) * step
    hann_window = np.float32(0.5) - np.float32(0.5) * np.cos(sample_num.astype(np.float32) * step)
    return np.stack([hann_window * np.cos(angles), -(hann_window * np.sin(angles))]).astype(jnp.bfloat16)


def spectra_kernel(
    starts_hbm, record_hbm, table_hbm, out_hbm,
    starts_ref, record_ref, table_ref, pieces_ref, out_ref, in_sem, table_sem, out_sem,
):
    chans, samples = record_ref.shape
    out_rows, seg_len = table_ref.shape
    segs = starts_ref.shape[0]
    wide = seg_len + LANES
    per_dot = 256 // chans
    starts_load = pltpu.make_async_copy(starts_hbm, starts_ref, in_sem.at[0])
    starts_load.start()
    ends = [min(samples, MAX_GAP * (first + per_dot - 1) + wide) for first in range(0, segs, per_dot)]
    loads, begin = [], 0
    for end in ends:
        part = pl.ds(begin, end - begin)
        loads.append(
            pltpu.make_async_copy(record_hbm.at[:, part], record_ref.at[:, part], in_sem.at[1 + len(loads)])
            if end > begin
            else None
        )
        begin = end
    row_blocks = [pl.ds(at, 256) for at in range(0, out_rows, 256)]
    tables = [
        pltpu.make_async_copy(table_hbm.at[rows], table_ref.at[rows], table_sem.at[k])
        for k, rows in enumerate(row_blocks)
    ]
    loads[0].start()
    tables[0].start()
    for load in loads[1:] + tables[1:]:
        if load is not None:
            load.start()
    lane = lax.broadcasted_iota(jnp.int32, (chans, LANES), 1)
    starts_load.wait()
    stores = []
    for row_block, rows in enumerate(row_blocks):
        for block, first in enumerate(range(0, segs, per_dot)):
            if row_block == 0:
                if loads[block] is not None:
                    loads[block].wait()
                for seg in range(first, first + per_dot):
                    start = starts_ref[seg]
                    base = jnp.minimum(start // LANES * LANES, samples - wide)
                    shift = start - base
                    back = LANES - shift
                    keep = lane < back
                    here = pl.ds(seg * chans, chans)
                    left = None
                    for tile in range(seg_len // LANES + 1):
                        at = pl.multiple_of(base + tile * LANES, LANES)
                        right = pltpu.roll(
                            record_ref[:, pl.ds(at, LANES)].astype(jnp.float32),
                            lax.rem(back, LANES),
                            1,
                        )
                        if tile:
                            pieces_ref[here, pl.ds((tile - 1) * LANES, LANES)] = jnp.where(
                                keep, left, right
                            ).astype(jnp.bfloat16)
                        left = right
            if block == 0:
                tables[row_block].wait()
            cols = pl.ds(first * chans, per_dot * chans)
            out_ref[rows, cols] = lax.dot_general(
                table_ref[rows, :],
                pieces_ref[cols, :],
                (((1,), (1,)), ((), ())),
                preferred_element_type=jnp.float32,
            ).astype(jnp.bfloat16)
        store = pltpu.make_async_copy(out_ref.at[rows], out_hbm.at[rows], out_sem.at[row_block])
        store.start()
        stores.append(store)
    for store in stores:
        store.wait()


def spectra_of(record, offsets, table):
    chans, samples = record.shape
    segs = offsets.shape[0]
    rows, seg_len = table.shape
    cols = segs * chans
    return pl.pallas_call(
        spectra_kernel,
        out_shape=jax.ShapeDtypeStruct((rows, cols), jnp.bfloat16),
        in_specs=[
            pl.BlockSpec(memory_space=pltpu.HBM),
            pl.BlockSpec(memory_space=pltpu.HBM),
            pl.BlockSpec(memory_space=pltpu.HBM),
        ],
        out_specs=pl.BlockSpec(memory_space=pltpu.HBM),
        scratch_shapes=[
            pltpu.SMEM((segs,), jnp.int32),
            pltpu.VMEM((chans, samples), jnp.bfloat16),
            pltpu.VMEM((rows, seg_len), jnp.bfloat16),
            pltpu.VMEM((cols, seg_len), jnp.bfloat16),
            pltpu.VMEM((rows, cols), jnp.bfloat16),
            pltpu.SemaphoreType.DMA((cols // 256 + 1,)),
            pltpu.SemaphoreType.DMA((rows // 256,)),
            pltpu.SemaphoreType.DMA((rows // 256,)),
        ],
        compiler_params=pltpu.CompilerParams(vmem_limit_bytes=SPECTRA_LIMIT),
        cost_estimate=pl.CostEstimate(
            flops=2 * rows * cols * seg_len, bytes_accessed=4 * rows * cols, transcendentals=0
        ),
        name="spectra",
    )(offsets, record, table)


def pick_kernel(index_ref, got_ref, out_ref):
    sources, rows, _ = got_ref.shape
    chans = LANES // 2
    group_rows = 2 * SUB
    tiles = got_ref.shape[2] // LANES
    index = index_ref[...]
    chan = lax.broadcasted_iota(jnp.int32, (LANES, LANES), 0)
    col = lax.broadcasted_iota(jnp.int32, (LANES, LANES), 1)
    same_seg = (chan >= chans) == (col >= chans)
    chan = jnp.where(chan >= chans, chan - chans, chan)
    picks = []
    for source in range(sources):
        hit = same_seg & (chan + source * chans == index)
        picks.append(jnp.where(hit, 1.0, 0.0).astype(jnp.bfloat16))
    for group in range(rows // group_rows):
        total = jnp.zeros((tiles * group_rows, LANES), jnp.float32)
        for source in range(sources):
            block = jnp.concatenate(
                [
                    got_ref[source, pl.ds(group * group_rows, group_rows), pl.ds(tile * LANES, LANES)]
                    for tile in range(tiles)
                ],
                axis=0,
            )
            total = total + jnp.dot(block, picks[source], preferred_element_type=jnp.float32)
        out_ref[group] = total.astype(jnp.bfloat16)


def pick_refs(index, got):
    sources, rows, cols = got.shape
    groups = rows // (2 * SUB)
    out_rows = cols // LANES * 2 * SUB
    return pl.pallas_call(
        pick_kernel,
        out_shape=jax.ShapeDtypeStruct((groups, out_rows, LANES), jnp.bfloat16),
        in_specs=[pl.BlockSpec(memory_space=pltpu.VMEM)] * 2,
        out_specs=pl.BlockSpec(memory_space=pltpu.VMEM),
        compiler_params=pltpu.CompilerParams(vmem_limit_bytes=VMEM_LIMIT),
        cost_estimate=pl.CostEstimate(
            flops=2 * groups * out_rows * sources * LANES * LANES,
            bytes_accessed=2 * sources * rows * cols,
            transcendentals=0,
        ),
        name="pick_refs",
    )(index, got)


def turn_kernel(got_ref, out_ref):
    sources, rows, _ = got_ref.shape
    chans = LANES // 2
    group_rows = 2 * SUB
    tiles = got_ref.shape[2] // LANES
    for group in range(rows // group_rows):
        for source in range(sources):
            block = jnp.concatenate(
                [
                    got_ref[source, pl.ds(group * group_rows, group_rows), pl.ds(tile * LANES, LANES)]
                    for tile in range(tiles)
                ],
                axis=0,
            )
            turned = block.T
            here = pl.ds(source * chans, chans)
            out_ref[group, here, 0:LANES] = turned[:chans]
            out_ref[group, here, LANES : 2 * LANES] = turned[chans:]


def turn(got):
    sources, rows, cols = got.shape
    groups = rows // (2 * SUB)
    return pl.pallas_call(
        turn_kernel,
        out_shape=jax.ShapeDtypeStruct((groups, sources * LANES // 2, 2 * LANES), jnp.bfloat16),
        in_specs=[pl.BlockSpec(memory_space=pltpu.VMEM)],
        out_specs=pl.BlockSpec(memory_space=pltpu.VMEM),
        compiler_params=pltpu.CompilerParams(vmem_limit_bytes=VMEM_LIMIT),
        cost_estimate=pl.CostEstimate(
            flops=0, bytes_accessed=4 * sources * rows * cols, transcendentals=0
        ),
        name="turn",
    )(got)


def solve_steps(refs, segs, total_refs, found):
    wide = refs[0][0].shape
    spread = lambda x: jnp.broadcast_to(x, wide)
    real, imag = {}, {}
    for i in range(segs):
        for j in range(i + 1):
            (ir, ii), (jr, ji) = refs[i], refs[j]
            real[i, j] = spread(jnp.sum(ir * jr + ii * ji, axis=1, keepdims=True))
            if i != j:
                imag[i, j] = spread(jnp.sum(ir * ji - ii * jr, axis=1, keepdims=True))
            yield 6
    trace = real[0, 0]
    for i in range(1, segs):
        trace = trace + real[i, i]
    ridge = ridge_weight * trace / total_refs
    for i in range(segs):
        real[i, i] = real[i, i] + ridge
    yield 2 * segs
    right = [(r, -i) for r, i in refs]
    lower = {}
    inverse = []
    for k in range(segs):
        inv = 1.0 / real[k, k]
        inverse.append(inv)
        for i in range(k + 1, segs):
            lower[i, k] = (real[i, k] * inv, imag[i, k] * inv)
        yield 8 + 2 * (segs - k)
        for i in range(k + 1, segs):
            lr, li = lower[i, k]
            for j in range(k + 1, i):
                gr, gi = real[j, k], imag[j, k]
                real[i, j] = real[i, j] - (lr * gr + li * gi)
                imag[i, j] = imag[i, j] - (li * gr - lr * gi)
            real[i, i] = real[i, i] - (lr * real[i, k] + li * imag[i, k])
            br, bi = right[k]
            cr, ci = right[i]
            right[i] = (cr - (lr * br - li * bi), ci - (lr * bi + li * br))
            yield 8 * (i - k - 1) + 12
    for k in range(segs - 1, -1, -1):
        br, bi = right[k]
        vr, vi = br * inverse[k], bi * inverse[k]
        for i in range(k + 1, segs):
            lr, li = lower[i, k]
            wr, wi = found[i]
            vr = vr - (lr * wr + li * wi)
            vi = vi - (lr * wi - li * wr)
        found[k] = (vr, vi)
        yield 2 + 8 * (segs - 1 - k)


def solve_kernel(own_ref, other_ref, turned_ref, out_hbm, wide_ref, slot_ref, sem):
    half = LANES // 2
    groups, rows, _ = own_ref.shape
    chans = turned_ref.shape[1]
    segs = 2 * rows // (2 * SUB)
    steps, pair = slot_ref.shape[:2]
    blocks = chans // 256
    first_half = lax.axis_index("grp") == 0
    row_bin = lax.broadcasted_iota(jnp.int32, wide_ref.shape[1:], 0) % SUB

    def copy_out(step, group):
        return pltpu.make_async_copy(
            slot_ref.at[step], out_hbm.at[pl.ds(group * SUB + step * pair, pair)], sem.at[step]
        )

    def solve(group, into):
        own = own_ref[group].astype(jnp.float32)
        other = other_ref[group].astype(jnp.float32)
        low = jnp.where(first_half, own, other)
        high = jnp.where(first_half, other, own)
        left = lax.broadcasted_iota(jnp.int32, low.shape, 1) < half
        even = jnp.where(left, low, pltpu.roll(high, half, 1))
        odd = jnp.where(left, pltpu.roll(low, half, 1), high)
        refs = []
        for seg in range(segs):
            source = odd if seg % 2 else even
            at = seg // 2 * 2 * SUB
            refs.append((source[at : at + SUB], source[at + SUB : at + 2 * SUB]))
        yield 100
        found = [None] * segs
        yield from solve_steps(refs, segs, LANES, found)
        for seg in range(segs):
            vr, vi = found[seg]
            at = (seg % 2) * LANES + seg // 2 * 2 * SUB
            wide_ref[into, at : at + SUB, 0:LANES] = vr
            wide_ref[into, at : at + SUB, LANES : 2 * LANES] = vi
            wide_ref[into, at + SUB : at + 2 * SUB, 0:LANES] = -vi
            wide_ref[into, at + SUB : at + 2 * SUB, LANES : 2 * LANES] = vr

    solve_cost = 100 + 6 * 136 + 32 + 8 * 16 + 240 + 8 * 560 + 12 * 120 + 32 + 960

    def apply(group, beside):
        done = 0
        for step in range(steps):
            copy_out(step, group).wait()
            weights = jnp.concatenate(
                [
                    jnp.where(row_bin == step * pair + k, wide_ref[group % 2], 0.0).astype(jnp.bfloat16)
                    for k in range(pair)
                ],
                axis=1,
            )
            for block in range(blocks):
                here = pl.ds(block * 256, 256)
                product = jnp.dot(
                    turned_ref[group, here, :], weights, preferred_element_type=jnp.float32
                ).astype(jnp.bfloat16)
                for k in range(pair):
                    slot_ref[step, k, here, :] = product[:, k * 2 * LANES : (k + 1) * 2 * LANES]
                limit = solve_cost * (step * blocks + block + 1) / (steps * blocks)
                while done < limit:
                    cost = next(beside, None)
                    if cost is None:
                        break
                    done += cost
            copy_out(step, group).start()
        for _ in beside:
            pass

    for step in range(steps):
        pltpu.make_async_copy(turned_ref.at[pl.ds(0, pair)], slot_ref.at[step], sem.at[step]).start()
    for _ in solve(0, 0):
        pass

    @pl.loop(0, groups - 1)
    def _(group):
        apply(group, solve(group + 1, (group + 1) % 2))

    apply(groups - 1, iter(()))
    for step in range(steps):
        copy_out(step, groups - 1).wait()


def solve_and_apply(own, other, turned):
    groups, chans, depth = turned.shape
    pair = 2
    steps = SUB // pair
    return pl.pallas_call(
        solve_kernel,
        out_shape=jax.ShapeDtypeStruct((groups * SUB, chans, 2 * LANES), jnp.bfloat16),
        in_specs=[pl.BlockSpec(memory_space=pltpu.VMEM)] * 3,
        out_specs=pl.BlockSpec(memory_space=pltpu.HBM),
        scratch_shapes=[
            pltpu.VMEM((2, depth, 2 * LANES), jnp.float32),
            pltpu.VMEM((steps, pair, chans, 2 * LANES), jnp.bfloat16),
            pltpu.SemaphoreType.DMA((steps,)),
        ],
        compiler_params=pltpu.CompilerParams(vmem_limit_bytes=VMEM_LIMIT),
        cost_estimate=pl.CostEstimate(
            flops=2 * groups * SUB * chans * depth * 2 * LANES,
            bytes_accessed=groups * SUB * chans * 4 * LANES,
            transcendentals=0,
        ),
        name="solve_apply",
    )(own, other, turned)


def local_kernels(record, ref_index, offsets):
    chan_rows = record[0]
    devices = lax.axis_size("bin")
    groups = NB // devices // SUB
    table = host_table(L, NB).reshape(2, devices, groups, SUB, L).transpose(1, 2, 0, 3, 4)
    index = jnp.concatenate([ref_index, ref_index], axis=1)
    sent = spectra_of(chan_rows, offsets, jnp.asarray(table.reshape(-1, L)))
    sent = sent.reshape(devices, groups * 2 * SUB, -1)
    got = lax.all_to_all(sent, "bin", 0, 0, tiled=True)
    own = pick_refs(index, got)
    other = lax.ppermute(own, "grp", [(0, 1), (1, 0)])
    turned = turn(got)
    return solve_and_apply(own, other, turned)


def transform(chan_rows, starts, dft_table, bin_devices):
    seg_len = dft_table.shape[0]
    pieces = jax.vmap(lambda start_at: lax.dynamic_slice_in_dim(chan_rows, start_at, seg_len, 1))(
        starts
    )
    spectra = jnp.einsum(
        "scn,nk->ksc", pieces, dft_table, preferred_element_type=jnp.float32
    ).astype(jnp.bfloat16)
    bin_total = dft_table.shape[1] // 2
    return spectra.reshape(
        2, bin_devices, bin_total // bin_devices, starts.shape[0], chan_rows.shape[0]
    )


def local(record, ref_index, offsets):
    chan_rows = record[0]
    dft_table = make_table(L, NB)
    bin_devices = lax.axis_size("bin")
    spectra = transform(chan_rows, offsets, dft_table, bin_devices)
    channels = lax.all_to_all(spectra, "bin", split_axis=1, concat_axis=4, tiled=True)[:, 0]
    local_refs = jnp.take(channels, ref_index[0], axis=3)
    references = lax.all_gather(local_refs, "grp", axis=3, tiled=True)
    ref_real = references[0]
    ref_imag = references[1]
    ref_blocks = jnp.stack(
        [
            jnp.concatenate([ref_real, -ref_imag], axis=-1),
            jnp.concatenate([ref_imag, ref_real], axis=-1),
        ]
    )
    bins_here = channels.shape[1]
    group_size = math.gcd(bins_here, 4)
    group_count = bins_here // group_size
    real_order = ref_blocks.shape[-1]

    def solve_bins(group_index):
        first_bin = group_index * group_size
        ref_group = lax.dynamic_slice_in_dim(ref_blocks, first_bin, group_size, 1)
        chan_group = lax.dynamic_slice_in_dim(channels, first_bin, group_size, 1)
        ref_rows = jnp.swapaxes(ref_group, 0, 1).reshape(group_size, -1, real_order)
        chan_cols = jnp.swapaxes(chan_group, 0, 1).reshape(group_size, -1, chan_group.shape[-1])
        gram_small = jnp.einsum(
            "fkr,fjr->fkj", ref_rows, ref_rows, preferred_element_type=jnp.float32
        )
        small_order = gram_small.shape[-1]
        ridge_term = ridge_weight * jnp.trace(gram_small, axis1=1, axis2=2) / real_order
        factor = jnp.linalg.cholesky(
            gram_small + ridge_term[:, None, None] * jnp.eye(small_order, dtype=jnp.float32)
        )
        solved = jax.scipy.linalg.cho_solve((factor, True), chan_cols.astype(jnp.float32))
        solved_high = solved.astype(jnp.bfloat16)
        solved_low = (solved - solved_high.astype(jnp.float32)).astype(jnp.bfloat16)
        transfer_t = jnp.einsum(
            "fkr,fkc->frc", ref_rows, solved_high, preferred_element_type=jnp.float32
        )
        transfer_t = transfer_t + jnp.einsum(
            "fkr,fkc->frc", ref_rows, solved_low, preferred_element_type=jnp.float32
        )
        return jnp.swapaxes(transfer_t, 1, 2).astype(jnp.bfloat16)

    results = lax.map(solve_bins, jnp.arange(group_count))
    return results.reshape(bins_here, results.shape[2], results.shape[3])


def solution(mesh):
    placed = (P("grp", "bin", None), P("grp", None), P())
    devices, groups = mesh.shape["bin"], mesh.shape["grp"]

    def whole(record, ref_index, offsets):
        chans = record.shape[1] // devices
        kernels = (
            groups == 2
            and 2 * chans == LANES
            and groups * ref_index.shape[1] == LANES
            and offsets.shape[0] == 2 * SUB
            and NB // devices % SUB == 0
        )
        return jax.shard_map(
            local_kernels if kernels else local,
            mesh=mesh,
            in_specs=placed,
            out_specs=P("bin", "grp", None),
            check_vma=False,
        )(record, ref_index, offsets)

    return whole
```

```python
import functools
import math

import jax
import jax.numpy as jnp
import numpy as np
from jax import lax
from jax.experimental import pallas as pl
from jax.experimental.pallas import tpu as pltpu
from jax.sharding import PartitionSpec as P

L = 1024
NB = 512
LANES = 128
SUB = 8
VMEM_LIMIT = 48 * 1024 * 1024
SPECTRA_LIMIT = 66000000
SHIFTS = (8, 1, 15, 4, 10, 2, 13, 5, 9, 3, 14, 6, 11, 7, 12)
FIRST = 4
LATE = 4
MAX_GAP = 768

ridge_weight = 0.5


def make_table(seg_len, bins):
    sample_num = lax.iota(jnp.int32, seg_len)[:, None]
    bin_num = lax.iota(jnp.int32, bins)[None, :]
    angles = (sample_num * bin_num % seg_len).astype(jnp.float32) * (2.0 * math.pi / seg_len)
    hann_window = 0.5 - 0.5 * jnp.cos(sample_num.astype(jnp.float32) * (2.0 * math.pi / seg_len))
    return jnp.concatenate(
        [hann_window * jnp.cos(angles), -(hann_window * jnp.sin(angles))], axis=1
    ).astype(jnp.bfloat16)


def host_table(seg_len, bins):
    step = np.float32(2.0 * math.pi / seg_len)
    sample_num = np.arange(seg_len, dtype=np.int64)
    bin_num = np.arange(bins, dtype=np.int64)[:, None]
    angles = (sample_num[None, :] * bin_num % seg_len).astype(np.float32) * step
    hann_window = np.float32(0.5) - np.float32(0.5) * np.cos(sample_num.astype(np.float32) * step)
    return np.stack([hann_window * np.cos(angles), -(hann_window * np.sin(angles))]).astype(jnp.bfloat16)


def spectra_kernel(dest_of, count, starts_hbm, record_hbm, table_hbm, *rest):
    outs_hbm = rest[:-8]
    starts_ref, record_ref, table_ref, pieces_ref, out_ref, in_sem, table_sem, out_sem = rest[-8:]
    chans, samples = record_ref.shape
    dest_rows, seg_len = table_ref.shape[1:]
    segs = starts_ref.shape[0]
    wide = seg_len + LANES
    per_dot = 256 // chans
    per_block = min(count, 256 // dest_rows)
    starts_load = pltpu.make_async_copy(starts_hbm, starts_ref, in_sem.at[0])
    starts_load.start()
    ends = [min(samples, MAX_GAP * (first + per_dot - 1) + wide) for first in range(0, segs, per_dot)]
    loads, begin = [starts_load], 0
    for end in ends:
        if end > begin:
            part = pl.ds(begin, end - begin)
            loads.append(
                pltpu.make_async_copy(record_hbm.at[:, part], record_ref.at[:, part], in_sem.at[len(loads)])
            )
            begin = end
    loads += [
        pltpu.make_async_copy(table_hbm.at[dest_of(k)], table_ref.at[k], table_sem.at[k])
        for k in range(count)
    ]
    for load in loads[1:]:
        load.start()
    for load in loads:
        load.wait()
    lane = lax.broadcasted_iota(jnp.int32, (chans, LANES), 1)
    for seg in range(segs):
        start = starts_ref[seg]
        base = jnp.minimum(start // LANES * LANES, samples - wide)
        shift = start - base
        back = LANES - shift
        keep = lane < back
        here = pl.ds(seg * chans, chans)
        left = None
        for tile in range(seg_len // LANES + 1):
            at = pl.multiple_of(base + tile * LANES, LANES)
            right = pltpu.roll(
                record_ref[:, pl.ds(at, LANES)].astype(jnp.float32), lax.rem(back, LANES), 1
            )
            if tile:
                pieces_ref[here, pl.ds((tile - 1) * LANES, LANES)] = jnp.where(
                    keep, left, right
                ).astype(jnp.bfloat16)
            left = right
    stores = []
    for first_dest in range(0, count, per_block):
        held = min(per_block, count - first_dest)
        rows = pl.ds(first_dest * dest_rows, held * dest_rows)
        for first in range(0, segs, per_dot):
            cols = pl.ds(first * chans, per_dot * chans)
            out_ref[rows, cols] = lax.dot_general(
                table_ref[pl.ds(first_dest, held)].reshape(held * dest_rows, seg_len),
                pieces_ref[cols, :],
                (((1,), (1,)), ((), ())),
                preferred_element_type=jnp.float32,
            ).astype(jnp.bfloat16)
        for k in range(first_dest, first_dest + held):
            rows = pl.ds(k * dest_rows, dest_rows)
            to = outs_hbm[k] if len(outs_hbm) > 1 else outs_hbm[0].at[k]
            stores.append(pltpu.make_async_copy(out_ref.at[rows], to, out_sem.at[k]))
            stores[-1].start()
    for store in stores:
        store.wait()


def spectra_of(record, offsets, table, dest_of, count, apart):
    chans, samples = record.shape
    segs = offsets.shape[0]
    dest_rows, seg_len = table.shape[1:]
    cols = segs * chans
    if apart:
        out_shape = [jax.ShapeDtypeStruct((dest_rows, cols), jnp.bfloat16)] * count
    else:
        out_shape = [jax.ShapeDtypeStruct((count, dest_rows, cols), jnp.bfloat16)]
    return pl.pallas_call(
        functools.partial(spectra_kernel, dest_of, count),
        out_shape=out_shape,
        in_specs=[pl.BlockSpec(memory_space=pltpu.HBM)] * 3,
        out_specs=[pl.BlockSpec(memory_space=pltpu.HBM)] * len(out_shape),
        scratch_shapes=[
            pltpu.SMEM((segs,), jnp.int32),
            pltpu.VMEM((chans, samples), jnp.bfloat16),
            pltpu.VMEM((count, dest_rows, seg_len), jnp.bfloat16),
            pltpu.VMEM((cols, seg_len), jnp.bfloat16),
            pltpu.VMEM((count * dest_rows, cols), jnp.bfloat16),
            pltpu.SemaphoreType.DMA((cols // 256 + 1,)),
            pltpu.SemaphoreType.DMA((count,)),
            pltpu.SemaphoreType.DMA((count,)),
        ],
        compiler_params=pltpu.CompilerParams(vmem_limit_bytes=SPECTRA_LIMIT),
        cost_estimate=pl.CostEstimate(
            flops=2 * count * dest_rows * cols * seg_len,
            bytes_accessed=4 * count * dest_rows * cols,
            transcendentals=0,
        ),
        name="spectra",
    )(offsets, record, table)


def stacked(ref, group):
    tiles = ref.shape[1] // LANES
    rows = pl.ds(group * 2 * SUB, 2 * SUB)
    return jnp.concatenate([ref[rows, pl.ds(tile * LANES, LANES)] for tile in range(tiles)], axis=0)


def pick_kernel(shifts, index_ref, *rest):
    out_ref = rest[-1]
    chans = LANES // 2
    groups = out_ref.shape[0]
    index = index_ref[...]
    chan = lax.broadcasted_iota(jnp.int32, (LANES, LANES), 0)
    col = lax.broadcasted_iota(jnp.int32, (LANES, LANES), 1)
    same_seg = (chan >= chans) == (col >= chans)
    chan = jnp.where(chan >= chans, chan - chans, chan)
    if len(rest) > len(shifts) + 1:
        totals = [rest[-2][group].astype(jnp.float32) for group in range(groups)]
    else:
        totals = [jnp.zeros(out_ref.shape[1:], jnp.float32)] * groups
    for shift, ref in zip(shifts, rest):
        source = lax.axis_index("bin") ^ shift
        hit = same_seg & (chan + source * chans == index)
        pick = jnp.where(hit, 1.0, 0.0).astype(jnp.bfloat16)
        for group in range(groups):
            totals[group] = totals[group] + jnp.dot(
                stacked(ref, group), pick, preferred_element_type=jnp.float32
            )
    for group in range(groups):
        out_ref[group] = totals[group].astype(jnp.bfloat16)


def pick_refs(index, shifts, got, before):
    rows, cols = got[0].shape
    groups = rows // (2 * SUB)
    out_rows = cols // LANES * 2 * SUB
    operands = [index, *got] + ([] if before is None else [before])
    return pl.pallas_call(
        functools.partial(pick_kernel, shifts),
        out_shape=jax.ShapeDtypeStruct((groups, out_rows, LANES), jnp.bfloat16),
        in_specs=[pl.BlockSpec(memory_space=pltpu.VMEM)] * len(operands),
        out_specs=pl.BlockSpec(memory_space=pltpu.VMEM),
        compiler_params=pltpu.CompilerParams(vmem_limit_bytes=VMEM_LIMIT),
        cost_estimate=pl.CostEstimate(
            flops=2 * len(got) * groups * out_rows * LANES * LANES,
            bytes_accessed=2 * len(got) * rows * cols,
            transcendentals=0,
        ),
        name="pick_refs",
    )(*operands)


def turn_kernel(*refs):
    out_ref = refs[-1]
    chans = LANES // 2
    for at, ref in enumerate(refs[:-1]):
        here = pl.ds(at * chans, chans)
        for group in range(out_ref.shape[0]):
            turned = stacked(ref, group).T
            out_ref[group, here, 0:LANES] = turned[:chans]
            out_ref[group, here, LANES : 2 * LANES] = turned[chans:]


def turn(got):
    rows, cols = got[0].shape
    groups = rows // (2 * SUB)
    return pl.pallas_call(
        turn_kernel,
        out_shape=jax.ShapeDtypeStruct((groups, len(got) * LANES // 2, 2 * LANES), jnp.bfloat16),
        in_specs=[pl.BlockSpec(memory_space=pltpu.VMEM)] * len(got),
        out_specs=pl.BlockSpec(memory_space=pltpu.VMEM),
        compiler_params=pltpu.CompilerParams(vmem_limit_bytes=VMEM_LIMIT),
        cost_estimate=pl.CostEstimate(
            flops=0, bytes_accessed=4 * len(got) * rows * cols, transcendentals=0
        ),
        name="turn",
    )(*got)


def solve_steps(refs, segs, total_refs, found):
    wide = refs[0][0].shape
    spread = lambda x: jnp.broadcast_to(x, wide)
    real, imag = {}, {}
    for i in range(segs):
        for j in range(i + 1):
            (ir, ii), (jr, ji) = refs[i], refs[j]
            real[i, j] = spread(jnp.sum(ir * jr + ii * ji, axis=1, keepdims=True))
            if i != j:
                imag[i, j] = spread(jnp.sum(ir * ji - ii * jr, axis=1, keepdims=True))
            yield 6
    trace = real[0, 0]
    for i in range(1, segs):
        trace = trace + real[i, i]
    ridge = ridge_weight * trace / total_refs
    for i in range(segs):
        real[i, i] = real[i, i] + ridge
    yield 2 * segs
    right = [(r, -i) for r, i in refs]
    lower = {}
    inverse = []
    for k in range(segs):
        inv = 1.0 / real[k, k]
        inverse.append(inv)
        for i in range(k + 1, segs):
            lower[i, k] = (real[i, k] * inv, imag[i, k] * inv)
        yield 8 + 2 * (segs - k)
        for i in range(k + 1, segs):
            lr, li = lower[i, k]
            for j in range(k + 1, i):
                gr, gi = real[j, k], imag[j, k]
                real[i, j] = real[i, j] - (lr * gr + li * gi)
                imag[i, j] = imag[i, j] - (li * gr - lr * gi)
            real[i, i] = real[i, i] - (lr * real[i, k] + li * imag[i, k])
            br, bi = right[k]
            cr, ci = right[i]
            right[i] = (cr - (lr * br - li * bi), ci - (lr * bi + li * br))
            yield 8 * (i - k - 1) + 12
    for k in range(segs - 1, -1, -1):
        br, bi = right[k]
        vr, vi = br * inverse[k], bi * inverse[k]
        for i in range(k + 1, segs):
            lr, li = lower[i, k]
            wr, wi = found[i]
            vr = vr - (lr * wr + li * wi)
            vi = vi - (lr * wi - li * wr)
        found[k] = (vr, vi)
        yield 2 + 8 * (segs - 1 - k)


def solve_kernel(shifts, own_ref, other_ref, early_ref, late_ref, out_hbm, wide_ref, slot_ref, sem):
    half = LANES // 2
    groups, rows, _ = own_ref.shape
    chans = LANES // 2
    early, late = early_ref.shape[1], late_ref.shape[1]
    segs = 2 * rows // (2 * SUB)
    steps, pair = slot_ref.shape[:2]
    blocks = [(early_ref, at) for at in range(0, early, 256)] + [(late_ref, at) for at in range(0, late, 256)]
    sources = [lax.axis_index("bin") ^ shift for shift in shifts]
    first_half = lax.axis_index("grp") == 0
    row_bin = lax.broadcasted_iota(jnp.int32, wide_ref.shape[1:], 0) % SUB

    def copy_out(step, group):
        return pltpu.make_async_copy(
            slot_ref.at[step], out_hbm.at[pl.ds(group * SUB + step * pair, pair)], sem.at[step]
        )

    def solve(group, into):
        own = own_ref[group].astype(jnp.float32)
        other = other_ref[group].astype(jnp.float32)
        low = jnp.where(first_half, own, other)
        high = jnp.where(first_half, other, own)
        left = lax.broadcasted_iota(jnp.int32, low.shape, 1) < half
        even = jnp.where(left, low, pltpu.roll(high, half, 1))
        odd = jnp.where(left, pltpu.roll(low, half, 1), high)
        refs = []
        for seg in range(segs):
            source = odd if seg % 2 else even
            at = seg // 2 * 2 * SUB
            refs.append((source[at : at + SUB], source[at + SUB : at + 2 * SUB]))
        yield 100
        found = [None] * segs
        yield from solve_steps(refs, segs, LANES, found)
        for seg in range(segs):
            vr, vi = found[seg]
            at = (seg % 2) * LANES + seg // 2 * 2 * SUB
            wide_ref[into, at : at + SUB, 0:LANES] = vr
            wide_ref[into, at : at + SUB, LANES : 2 * LANES] = vi
            wide_ref[into, at + SUB : at + 2 * SUB, 0:LANES] = -vi
            wide_ref[into, at + SUB : at + 2 * SUB, LANES : 2 * LANES] = vr

    solve_cost = 100 + 6 * 136 + 32 + 8 * 16 + 240 + 8 * 560 + 12 * 120 + 32 + 960

    def apply(group, beside):
        done = 0
        for step in range(steps):
            copy_out(step, group).wait()
            weights = jnp.concatenate(
                [
                    jnp.where(row_bin == step * pair + k, wide_ref[group % 2], 0.0).astype(jnp.bfloat16)
                    for k in range(pair)
                ],
                axis=1,
            )
            for block, (turned_ref, first) in enumerate(blocks):
                product = jnp.dot(
                    turned_ref[group, pl.ds(first, 256), :], weights, preferred_element_type=jnp.float32
                ).astype(jnp.bfloat16)
                for at in range(0, 256, chans):
                    source = sources[(block * 256 + at) // chans]
                    here = pl.ds(pl.multiple_of(source * chans, chans), chans)
                    for k in range(pair):
                        slot_ref[step, k, here, :] = product[
                            at : at + chans, k * 2 * LANES : (k + 1) * 2 * LANES
                        ]
                limit = solve_cost * (step * len(blocks) + block + 1) / (steps * len(blocks))
                while done < limit:
                    cost = next(beside, None)
                    if cost is None:
                        break
                    done += cost
            copy_out(step, group).start()
        for _ in beside:
            pass

    for step in range(steps):
        for ref, rows in ((early_ref, pl.ds(0, early)), (late_ref, pl.ds(early, late))):
            pltpu.make_async_copy(
                ref.at[pl.ds(0, pair)], slot_ref.at[step, :, rows], sem.at[step]
            ).start()
    for _ in solve(0, 0):
        pass

    @pl.loop(0, groups - 1)
    def _(group):
        apply(group, solve(group + 1, (group + 1) % 2))

    apply(groups - 1, iter(()))
    for step in range(steps):
        copy_out(step, groups - 1).wait()


def solve_and_apply(shifts, own, other, early, late):
    groups, _, depth = early.shape
    chans = early.shape[1] + late.shape[1]
    pair = 2
    steps = SUB // pair
    return pl.pallas_call(
        functools.partial(solve_kernel, shifts),
        out_shape=jax.ShapeDtypeStruct((groups * SUB, chans, 2 * LANES), jnp.bfloat16),
        in_specs=[pl.BlockSpec(memory_space=pltpu.VMEM)] * 4,
        out_specs=pl.BlockSpec(memory_space=pltpu.HBM),
        scratch_shapes=[
            pltpu.VMEM((2, depth, 2 * LANES), jnp.float32),
            pltpu.VMEM((steps, pair, chans, 2 * LANES), jnp.bfloat16),
            pltpu.SemaphoreType.DMA((steps,)),
        ],
        compiler_params=pltpu.CompilerParams(vmem_limit_bytes=VMEM_LIMIT),
        cost_estimate=pl.CostEstimate(
            flops=2 * groups * SUB * chans * depth * 2 * LANES,
            bytes_accessed=groups * SUB * chans * 4 * LANES,
            transcendentals=0,
        ),
        name="solve_apply",
    )(own, other, early, late)


def local_kernels(record, ref_index, offsets):
    chan_rows = record[0]
    devices = lax.axis_size("bin")
    groups = NB // devices // SUB
    table = host_table(L, NB).reshape(2, devices, groups, SUB, L).transpose(1, 2, 0, 3, 4)
    table = jnp.asarray(table.reshape(devices, -1, L))
    index = jnp.concatenate([ref_index, ref_index], axis=1)
    me = lambda: lax.axis_index("bin")
    got = {}
    for part in (SHIFTS[:FIRST], SHIFTS[FIRST:] + (0,)):
        made = spectra_of(
            chan_rows, offsets, table, lambda k, part=part: me() ^ part[k], len(part), True
        )
        chan_rows, *made = lax.optimization_barrier((chan_rows, *made))
        for shift, block in zip(part, made):
            pairs = [(i, i ^ shift) for i in range(devices)]
            got[shift] = lax.ppermute(block, "bin", pairs) if shift else block
    early, late = (0,) + SHIFTS[:-LATE], SHIFTS[-LATE:]
    got_early, got_late = [got[shift] for shift in early], [got[shift] for shift in late]
    own = pick_refs(index, late, got_late, pick_refs(index, early, got_early, None))
    other = lax.ppermute(own, "grp", [(0, 1), (1, 0)])
    return solve_and_apply(early + late, own, other, turn(got_early), turn(got_late))


def transform(chan_rows, starts, dft_table, bin_devices):
    seg_len = dft_table.shape[0]
    pieces = jax.vmap(lambda start_at: lax.dynamic_slice_in_dim(chan_rows, start_at, seg_len, 1))(
        starts
    )
    spectra = jnp.einsum(
        "scn,nk->ksc", pieces, dft_table, preferred_element_type=jnp.float32
    ).astype(jnp.bfloat16)
    bin_total = dft_table.shape[1] // 2
    return spectra.reshape(
        2, bin_devices, bin_total // bin_devices, starts.shape[0], chan_rows.shape[0]
    )


def local(record, ref_index, offsets):
    chan_rows = record[0]
    dft_table = make_table(L, NB)
    bin_devices = lax.axis_size("bin")
    spectra = transform(chan_rows, offsets, dft_table, bin_devices)
    channels = lax.all_to_all(spectra, "bin", split_axis=1, concat_axis=4, tiled=True)[:, 0]
    local_refs = jnp.take(channels, ref_index[0], axis=3)
    references = lax.all_gather(local_refs, "grp", axis=3, tiled=True)
    ref_real = references[0]
    ref_imag = references[1]
    ref_blocks = jnp.stack(
        [
            jnp.concatenate([ref_real, -ref_imag], axis=-1),
            jnp.concatenate([ref_imag, ref_real], axis=-1),
        ]
    )
    bins_here = channels.shape[1]
    group_size = math.gcd(bins_here, 4)
    group_count = bins_here // group_size
    real_order = ref_blocks.shape[-1]

    def solve_bins(group_index):
        first_bin = group_index * group_size
        ref_group = lax.dynamic_slice_in_dim(ref_blocks, first_bin, group_size, 1)
        chan_group = lax.dynamic_slice_in_dim(channels, first_bin, group_size, 1)
        ref_rows = jnp.swapaxes(ref_group, 0, 1).reshape(group_size, -1, real_order)
        chan_cols = jnp.swapaxes(chan_group, 0, 1).reshape(group_size, -1, chan_group.shape[-1])
        gram_small = jnp.einsum(
            "fkr,fjr->fkj", ref_rows, ref_rows, preferred_element_type=jnp.float32
        )
        small_order = gram_small.shape[-1]
        ridge_term = ridge_weight * jnp.trace(gram_small, axis1=1, axis2=2) / real_order
        factor = jnp.linalg.cholesky(
            gram_small + ridge_term[:, None, None] * jnp.eye(small_order, dtype=jnp.float32)
        )
        solved = jax.scipy.linalg.cho_solve((factor, True), chan_cols.astype(jnp.float32))
        solved_high = solved.astype(jnp.bfloat16)
        solved_low = (solved - solved_high.astype(jnp.float32)).astype(jnp.bfloat16)
        transfer_t = jnp.einsum(
            "fkr,fkc->frc", ref_rows, solved_high, preferred_element_type=jnp.float32
        )
        transfer_t = transfer_t + jnp.einsum(
            "fkr,fkc->frc", ref_rows, solved_low, preferred_element_type=jnp.float32
        )
        return jnp.swapaxes(transfer_t, 1, 2).astype(jnp.bfloat16)

    results = lax.map(solve_bins, jnp.arange(group_count))
    return results.reshape(bins_here, results.shape[2], results.shape[3])


def solution(mesh):
    placed = (P("grp", "bin", None), P("grp", None), P())
    devices, groups = mesh.shape["bin"], mesh.shape["grp"]

    def whole(record, ref_index, offsets):
        chans = record.shape[1] // devices
        kernels = (
            devices == 1 + len(SHIFTS)
            and groups == 2
            and 2 * chans == LANES
            and groups * ref_index.shape[1] == LANES
            and offsets.shape[0] == 2 * SUB
            and NB // devices % SUB == 0
            and NB // devices >= 2 * SUB
        )
        return jax.shard_map(
            local_kernels if kernels else local,
            mesh=mesh,
            in_specs=placed,
            out_specs=P("bin", "grp", None),
            check_vma=False,
        )(record, ref_index, offsets)

    return whole
```

```python
import functools
import math

import jax
import jax.numpy as jnp
import numpy as np
from jax import lax
from jax.experimental import pallas as pl
from jax.experimental.pallas import tpu as pltpu
from jax.sharding import PartitionSpec as P

L = 1024
NB = 512
LANES = 128
SUB = 8
VMEM_LIMIT = 48 * 1024 * 1024
SPECTRA_LIMIT = 66000000
SHIFTS = (12, 7, 9, 4, 10, 5, 15, 1, 13, 2, 11, 6, 14, 3, 8)
FIRST = 3
LATE = 4
MAX_GAP = 768

ridge_weight = 0.5


def make_table(seg_len, bins):
    sample_num = lax.iota(jnp.int32, seg_len)[:, None]
    bin_num = lax.iota(jnp.int32, bins)[None, :]
    angles = (sample_num * bin_num % seg_len).astype(jnp.float32) * (2.0 * math.pi / seg_len)
    hann_window = 0.5 - 0.5 * jnp.cos(sample_num.astype(jnp.float32) * (2.0 * math.pi / seg_len))
    return jnp.concatenate(
        [hann_window * jnp.cos(angles), -(hann_window * jnp.sin(angles))], axis=1
    ).astype(jnp.bfloat16)


def host_table(seg_len, bins):
    step = np.float32(2.0 * math.pi / seg_len)
    sample_num = np.arange(seg_len, dtype=np.int64)
    bin_num = np.arange(bins, dtype=np.int64)[:, None]
    angles = (sample_num[None, :] * bin_num % seg_len).astype(np.float32) * step
    hann_window = np.float32(0.5) - np.float32(0.5) * np.cos(sample_num.astype(np.float32) * step)
    return np.stack([hann_window * np.cos(angles), -(hann_window * np.sin(angles))]).astype(jnp.bfloat16)


def spectra_kernel(dest_of, count, starts_hbm, record_hbm, table_hbm, *rest):
    outs_hbm = rest[:-8]
    starts_ref, record_ref, table_ref, pieces_ref, out_ref, in_sem, table_sem, out_sem = rest[-8:]
    chans, samples = record_ref.shape
    dest_rows, seg_len = table_ref.shape[1:]
    segs = starts_ref.shape[0]
    wide = seg_len + LANES
    per_dot = 256 // chans
    per_block = min(count, 256 // dest_rows)
    starts_load = pltpu.make_async_copy(starts_hbm, starts_ref, in_sem.at[0])
    starts_load.start()
    ends = [min(samples, MAX_GAP * (first + per_dot - 1) + wide) for first in range(0, segs, per_dot)]
    loads, begin = [starts_load], 0
    for end in ends:
        if end > begin:
            part = pl.ds(begin, end - begin)
            loads.append(
                pltpu.make_async_copy(record_hbm.at[:, part], record_ref.at[:, part], in_sem.at[len(loads)])
            )
            begin = end
    loads += [
        pltpu.make_async_copy(table_hbm.at[dest_of(k)], table_ref.at[k], table_sem.at[k])
        for k in range(count)
    ]
    for load in loads[1:]:
        load.start()
    for load in loads:
        load.wait()
    lane = lax.broadcasted_iota(jnp.int32, (chans, LANES), 1)
    for seg in range(segs):
        start = starts_ref[seg]
        base = jnp.minimum(start // LANES * LANES, samples - wide)
        shift = start - base
        back = LANES - shift
        keep = lane < back
        here = pl.ds(seg * chans, chans)
        left = None
        for tile in range(seg_len // LANES + 1):
            at = pl.multiple_of(base + tile * LANES, LANES)
            right = pltpu.roll(
                record_ref[:, pl.ds(at, LANES)].astype(jnp.float32), lax.rem(back, LANES), 1
            )
            if tile:
                pieces_ref[here, pl.ds((tile - 1) * LANES, LANES)] = jnp.where(
                    keep, left, right
                ).astype(jnp.bfloat16)
            left = right
    stores = []
    for first_dest in range(0, count, per_block):
        held = min(per_block, count - first_dest)
        rows = pl.ds(first_dest * dest_rows, held * dest_rows)
        for first in range(0, segs, per_dot):
            cols = pl.ds(first * chans, per_dot * chans)
            out_ref[rows, cols] = lax.dot_general(
                table_ref[pl.ds(first_dest, held)].reshape(held * dest_rows, seg_len),
                pieces_ref[cols, :],
                (((1,), (1,)), ((), ())),
                preferred_element_type=jnp.float32,
            ).astype(jnp.bfloat16)
        for k in range(first_dest, first_dest + held):
            rows = pl.ds(k * dest_rows, dest_rows)
            to = outs_hbm[k] if len(outs_hbm) > 1 else outs_hbm[0].at[k]
            stores.append(pltpu.make_async_copy(out_ref.at[rows], to, out_sem.at[k]))
            stores[-1].start()
    for store in stores:
        store.wait()


def spectra_of(record, offsets, table, dest_of, count, apart):
    chans, samples = record.shape
    segs = offsets.shape[0]
    dest_rows, seg_len = table.shape[1:]
    cols = segs * chans
    if apart:
        out_shape = [jax.ShapeDtypeStruct((dest_rows, cols), jnp.bfloat16)] * count
    else:
        out_shape = [jax.ShapeDtypeStruct((count, dest_rows, cols), jnp.bfloat16)]
    return pl.pallas_call(
        functools.partial(spectra_kernel, dest_of, count),
        out_shape=out_shape,
        in_specs=[pl.BlockSpec(memory_space=pltpu.HBM)] * 3,
        out_specs=[pl.BlockSpec(memory_space=pltpu.HBM)] * len(out_shape),
        scratch_shapes=[
            pltpu.SMEM((segs,), jnp.int32),
            pltpu.VMEM((chans, samples), jnp.bfloat16),
            pltpu.VMEM((count, dest_rows, seg_len), jnp.bfloat16),
            pltpu.VMEM((cols, seg_len), jnp.bfloat16),
            pltpu.VMEM((count * dest_rows, cols), jnp.bfloat16),
            pltpu.SemaphoreType.DMA((cols // 256 + 1,)),
            pltpu.SemaphoreType.DMA((count,)),
            pltpu.SemaphoreType.DMA((count,)),
        ],
        compiler_params=pltpu.CompilerParams(vmem_limit_bytes=SPECTRA_LIMIT),
        cost_estimate=pl.CostEstimate(
            flops=2 * count * dest_rows * cols * seg_len,
            bytes_accessed=4 * count * dest_rows * cols,
            transcendentals=0,
        ),
        name="spectra",
    )(offsets, record, table)


def stacked(ref, group):
    tiles = ref.shape[1] // LANES
    rows = pl.ds(group * 2 * SUB, 2 * SUB)
    return jnp.concatenate([ref[rows, pl.ds(tile * LANES, LANES)] for tile in range(tiles)], axis=0)


def pick_kernel(shifts, index_ref, *rest):
    out_ref = rest[-1]
    chans = LANES // 2
    groups = out_ref.shape[0]
    index = index_ref[...]
    chan = lax.broadcasted_iota(jnp.int32, (LANES, LANES), 0)
    col = lax.broadcasted_iota(jnp.int32, (LANES, LANES), 1)
    same_seg = (chan >= chans) == (col >= chans)
    chan = jnp.where(chan >= chans, chan - chans, chan)
    if len(rest) > len(shifts) + 1:
        totals = [rest[-2][group].astype(jnp.float32) for group in range(groups)]
    else:
        totals = [jnp.zeros(out_ref.shape[1:], jnp.float32)] * groups
    for shift, ref in zip(shifts, rest):
        source = lax.axis_index("bin") ^ shift
        hit = same_seg & (chan + source * chans == index)
        pick = jnp.where(hit, 1.0, 0.0).astype(jnp.bfloat16)
        for group in range(groups):
            totals[group] = totals[group] + jnp.dot(
                stacked(ref, group), pick, preferred_element_type=jnp.float32
            )
    for group in range(groups):
        out_ref[group] = totals[group].astype(jnp.bfloat16)


def pick_refs(index, shifts, got, before):
    rows, cols = got[0].shape
    groups = rows // (2 * SUB)
    out_rows = cols // LANES * 2 * SUB
    operands = [index, *got] + ([] if before is None else [before])
    return pl.pallas_call(
        functools.partial(pick_kernel, shifts),
        out_shape=jax.ShapeDtypeStruct((groups, out_rows, LANES), jnp.bfloat16),
        in_specs=[pl.BlockSpec(memory_space=pltpu.VMEM)] * len(operands),
        out_specs=pl.BlockSpec(memory_space=pltpu.VMEM),
        compiler_params=pltpu.CompilerParams(vmem_limit_bytes=VMEM_LIMIT),
        cost_estimate=pl.CostEstimate(
            flops=2 * len(got) * groups * out_rows * LANES * LANES,
            bytes_accessed=2 * len(got) * rows * cols,
            transcendentals=0,
        ),
        name="pick_refs",
    )(*operands)


def turn_kernel(*refs):
    out_ref = refs[-1]
    chans = LANES // 2
    for at, ref in enumerate(refs[:-1]):
        here = pl.ds(at * chans, chans)
        for group in range(out_ref.shape[0]):
            turned = stacked(ref, group).T
            out_ref[group, here, 0:LANES] = turned[:chans]
            out_ref[group, here, LANES : 2 * LANES] = turned[chans:]


def turn(got):
    rows, cols = got[0].shape
    groups = rows // (2 * SUB)
    return pl.pallas_call(
        turn_kernel,
        out_shape=jax.ShapeDtypeStruct((groups, len(got) * LANES // 2, 2 * LANES), jnp.bfloat16),
        in_specs=[pl.BlockSpec(memory_space=pltpu.VMEM)] * len(got),
        out_specs=pl.BlockSpec(memory_space=pltpu.VMEM),
        compiler_params=pltpu.CompilerParams(vmem_limit_bytes=VMEM_LIMIT),
        cost_estimate=pl.CostEstimate(
            flops=0, bytes_accessed=4 * len(got) * rows * cols, transcendentals=0
        ),
        name="turn",
    )(*got)


def solve_steps(refs, segs, total_refs, found):
    wide = refs[0][0].shape
    spread = lambda x: jnp.broadcast_to(x, wide)
    real, imag = {}, {}
    for i in range(segs):
        for j in range(i + 1):
            (ir, ii), (jr, ji) = refs[i], refs[j]
            real[i, j] = spread(jnp.sum(ir * jr + ii * ji, axis=1, keepdims=True))
            if i != j:
                imag[i, j] = spread(jnp.sum(ir * ji - ii * jr, axis=1, keepdims=True))
            yield 6
    trace = real[0, 0]
    for i in range(1, segs):
        trace = trace + real[i, i]
    ridge = ridge_weight * trace / total_refs
    for i in range(segs):
        real[i, i] = real[i, i] + ridge
    yield 2 * segs
    right = [(r, -i) for r, i in refs]
    lower = {}
    inverse = []
    for k in range(segs):
        inv = 1.0 / real[k, k]
        inverse.append(inv)
        for i in range(k + 1, segs):
            lower[i, k] = (real[i, k] * inv, imag[i, k] * inv)
        yield 8 + 2 * (segs - k)
        for i in range(k + 1, segs):
            lr, li = lower[i, k]
            for j in range(k + 1, i):
                gr, gi = real[j, k], imag[j, k]
                real[i, j] = real[i, j] - (lr * gr + li * gi)
                imag[i, j] = imag[i, j] - (li * gr - lr * gi)
            real[i, i] = real[i, i] - (lr * real[i, k] + li * imag[i, k])
            br, bi = right[k]
            cr, ci = right[i]
            right[i] = (cr - (lr * br - li * bi), ci - (lr * bi + li * br))
            yield 8 * (i - k - 1) + 12
    for k in range(segs - 1, -1, -1):
        br, bi = right[k]
        vr, vi = br * inverse[k], bi * inverse[k]
        for i in range(k + 1, segs):
            lr, li = lower[i, k]
            wr, wi = found[i]
            vr = vr - (lr * wr + li * wi)
            vi = vi - (lr * wi - li * wr)
        found[k] = (vr, vi)
        yield 2 + 8 * (segs - 1 - k)


def solve_kernel(shifts, own_ref, other_ref, early_ref, late_ref, out_hbm, wide_ref, slot_ref, sem):
    half = LANES // 2
    groups, rows, _ = own_ref.shape
    chans = LANES // 2
    early, late = early_ref.shape[1], late_ref.shape[1]
    segs = 2 * rows // (2 * SUB)
    steps, pair = slot_ref.shape[:2]
    blocks = [(early_ref, at) for at in range(0, early, 256)] + [(late_ref, at) for at in range(0, late, 256)]
    sources = [lax.axis_index("bin") ^ shift for shift in shifts]
    first_half = lax.axis_index("grp") == 0
    row_bin = lax.broadcasted_iota(jnp.int32, wide_ref.shape[1:], 0) % SUB

    def copy_out(step, group):
        return pltpu.make_async_copy(
            slot_ref.at[step], out_hbm.at[pl.ds(group * SUB + step * pair, pair)], sem.at[step]
        )

    def solve(group, into):
        own = own_ref[group].astype(jnp.float32)
        other = other_ref[group].astype(jnp.float32)
        low = jnp.where(first_half, own, other)
        high = jnp.where(first_half, other, own)
        left = lax.broadcasted_iota(jnp.int32, low.shape, 1) < half
        even = jnp.where(left, low, pltpu.roll(high, half, 1))
        odd = jnp.where(left, pltpu.roll(low, half, 1), high)
        refs = []
        for seg in range(segs):
            source = odd if seg % 2 else even
            at = seg // 2 * 2 * SUB
            refs.append((source[at : at + SUB], source[at + SUB : at + 2 * SUB]))
        yield 100
        found = [None] * segs
        yield from solve_steps(refs, segs, LANES, found)
        for seg in range(segs):
            vr, vi = found[seg]
            at = (seg % 2) * LANES + seg // 2 * 2 * SUB
            wide_ref[into, at : at + SUB, 0:LANES] = vr
            wide_ref[into, at : at + SUB, LANES : 2 * LANES] = vi
            wide_ref[into, at + SUB : at + 2 * SUB, 0:LANES] = -vi
            wide_ref[into, at + SUB : at + 2 * SUB, LANES : 2 * LANES] = vr

    solve_cost = 100 + 6 * 136 + 32 + 8 * 16 + 240 + 8 * 560 + 12 * 120 + 32 + 960

    def apply(group, beside):
        done = 0
        for step in range(steps):
            copy_out(step, group).wait()
            weights = jnp.concatenate(
                [
                    jnp.where(row_bin == step * pair + k, wide_ref[group % 2], 0.0).astype(jnp.bfloat16)
                    for k in range(pair)
                ],
                axis=1,
            )
            for block, (turned_ref, first) in enumerate(blocks):
                product = jnp.dot(
                    turned_ref[group, pl.ds(first, 256), :], weights, preferred_element_type=jnp.float32
                ).astype(jnp.bfloat16)
                for at in range(0, 256, chans):
                    source = sources[(block * 256 + at) // chans]
                    here = pl.ds(pl.multiple_of(source * chans, chans), chans)
                    for k in range(pair):
                        slot_ref[step, k, here, :] = product[
                            at : at + chans, k * 2 * LANES : (k + 1) * 2 * LANES
                        ]
                limit = solve_cost * (step * len(blocks) + block + 1) / (steps * len(blocks))
                while done < limit:
                    cost = next(beside, None)
                    if cost is None:
                        break
                    done += cost
            copy_out(step, group).start()
        for _ in beside:
            pass

    for step in range(steps):
        for ref, rows in ((early_ref, pl.ds(0, early)), (late_ref, pl.ds(early, late))):
            pltpu.make_async_copy(
                ref.at[pl.ds(0, pair)], slot_ref.at[step, :, rows], sem.at[step]
            ).start()
    for _ in solve(0, 0):
        pass

    @pl.loop(0, groups - 1)
    def _(group):
        apply(group, solve(group + 1, (group + 1) % 2))

    apply(groups - 1, iter(()))
    for step in range(steps):
        copy_out(step, groups - 1).wait()


def solve_and_apply(shifts, own, other, early, late):
    groups, _, depth = early.shape
    chans = early.shape[1] + late.shape[1]
    pair = 2
    steps = SUB // pair
    return pl.pallas_call(
        functools.partial(solve_kernel, shifts),
        out_shape=jax.ShapeDtypeStruct((groups * SUB, chans, 2 * LANES), jnp.bfloat16),
        in_specs=[pl.BlockSpec(memory_space=pltpu.VMEM)] * 4,
        out_specs=pl.BlockSpec(memory_space=pltpu.HBM),
        scratch_shapes=[
            pltpu.VMEM((2, depth, 2 * LANES), jnp.float32),
            pltpu.VMEM((steps, pair, chans, 2 * LANES), jnp.bfloat16),
            pltpu.SemaphoreType.DMA((steps,)),
        ],
        compiler_params=pltpu.CompilerParams(vmem_limit_bytes=VMEM_LIMIT),
        cost_estimate=pl.CostEstimate(
            flops=2 * groups * SUB * chans * depth * 2 * LANES,
            bytes_accessed=groups * SUB * chans * 4 * LANES,
            transcendentals=0,
        ),
        name="solve_apply",
    )(own, other, early, late)


def local_kernels(record, ref_index, offsets):
    chan_rows = record[0]
    devices = lax.axis_size("bin")
    groups = NB // devices // SUB
    table = host_table(L, NB).reshape(2, devices, groups, SUB, L).transpose(1, 2, 0, 3, 4)
    table = jnp.asarray(table.reshape(devices, -1, L))
    index = jnp.concatenate([ref_index, ref_index], axis=1)
    me = lambda: lax.axis_index("bin")
    got = {}
    for part in (SHIFTS[:FIRST], SHIFTS[FIRST:] + (0,)):
        made = spectra_of(
            chan_rows, offsets, table, lambda k, part=part: me() ^ part[k], len(part), True
        )
        chan_rows, *made = lax.optimization_barrier((chan_rows, *made))
        for shift, block in zip(part, made):
            pairs = [(i, i ^ shift) for i in range(devices)]
            got[shift] = lax.ppermute(block, "bin", pairs) if shift else block
    early, late = (0,) + SHIFTS[:-LATE], SHIFTS[-LATE:]
    got_early, got_late = [got[shift] for shift in early], [got[shift] for shift in late]
    own = pick_refs(index, late, got_late, pick_refs(index, early, got_early, None))
    other = lax.ppermute(own, "grp", [(0, 1), (1, 0)])
    return solve_and_apply(early + late, own, other, turn(got_early), turn(got_late))


def transform(chan_rows, starts, dft_table, bin_devices):
    seg_len = dft_table.shape[0]
    pieces = jax.vmap(lambda start_at: lax.dynamic_slice_in_dim(chan_rows, start_at, seg_len, 1))(
        starts
    )
    spectra = jnp.einsum(
        "scn,nk->ksc", pieces, dft_table, preferred_element_type=jnp.float32
    ).astype(jnp.bfloat16)
    bin_total = dft_table.shape[1] // 2
    return spectra.reshape(
        2, bin_devices, bin_total // bin_devices, starts.shape[0], chan_rows.shape[0]
    )


def local(record, ref_index, offsets):
    chan_rows = record[0]
    dft_table = make_table(L, NB)
    bin_devices = lax.axis_size("bin")
    spectra = transform(chan_rows, offsets, dft_table, bin_devices)
    channels = lax.all_to_all(spectra, "bin", split_axis=1, concat_axis=4, tiled=True)[:, 0]
    local_refs = jnp.take(channels, ref_index[0], axis=3)
    references = lax.all_gather(local_refs, "grp", axis=3, tiled=True)
    ref_real = references[0]
    ref_imag = references[1]
    ref_blocks = jnp.stack(
        [
            jnp.concatenate([ref_real, -ref_imag], axis=-1),
            jnp.concatenate([ref_imag, ref_real], axis=-1),
        ]
    )
    bins_here = channels.shape[1]
    group_size = math.gcd(bins_here, 4)
    group_count = bins_here // group_size
    real_order = ref_blocks.shape[-1]

    def solve_bins(group_index):
        first_bin = group_index * group_size
        ref_group = lax.dynamic_slice_in_dim(ref_blocks, first_bin, group_size, 1)
        chan_group = lax.dynamic_slice_in_dim(channels, first_bin, group_size, 1)
        ref_rows = jnp.swapaxes(ref_group, 0, 1).reshape(group_size, -1, real_order)
        chan_cols = jnp.swapaxes(chan_group, 0, 1).reshape(group_size, -1, chan_group.shape[-1])
        gram_small = jnp.einsum(
            "fkr,fjr->fkj", ref_rows, ref_rows, preferred_element_type=jnp.float32
        )
        small_order = gram_small.shape[-1]
        ridge_term = ridge_weight * jnp.trace(gram_small, axis1=1, axis2=2) / real_order
        factor = jnp.linalg.cholesky(
            gram_small + ridge_term[:, None, None] * jnp.eye(small_order, dtype=jnp.float32)
        )
        solved = jax.scipy.linalg.cho_solve((factor, True), chan_cols.astype(jnp.float32))
        solved_high = solved.astype(jnp.bfloat16)
        solved_low = (solved - solved_high.astype(jnp.float32)).astype(jnp.bfloat16)
        transfer_t = jnp.einsum(
            "fkr,fkc->frc", ref_rows, solved_high, preferred_element_type=jnp.float32
        )
        transfer_t = transfer_t + jnp.einsum(
            "fkr,fkc->frc", ref_rows, solved_low, preferred_element_type=jnp.float32
        )
        return jnp.swapaxes(transfer_t, 1, 2).astype(jnp.bfloat16)

    results = lax.map(solve_bins, jnp.arange(group_count))
    return results.reshape(bins_here, results.shape[2], results.shape[3])


def solution(mesh):
    placed = (P("grp", "bin", None), P("grp", None), P())
    devices, groups = mesh.shape["bin"], mesh.shape["grp"]

    def whole(record, ref_index, offsets):
        chans = record.shape[1] // devices
        kernels = (
            devices == 1 + len(SHIFTS)
            and groups == 2
            and 2 * chans == LANES
            and groups * ref_index.shape[1] == LANES
            and offsets.shape[0] == 2 * SUB
            and NB // devices % SUB == 0
            and NB // devices >= 2 * SUB
        )
        return jax.shard_map(
            local_kernels if kernels else local,
            mesh=mesh,
            in_specs=placed,
            out_specs=P("bin", "grp", None),
            check_vma=False,
        )(record, ref_index, offsets)

    return whole
```

```python
import functools
import math

import jax
import jax.numpy as jnp
import numpy as np
from jax import lax
from jax.experimental import pallas as pl
from jax.experimental.pallas import tpu as pltpu
from jax.sharding import PartitionSpec as P

L = 1024
NB = 512
LANES = 128
SUB = 8
VMEM_LIMIT = 48 * 1024 * 1024
SPECTRA_LIMIT = 66000000
SHIFTS = (12, 1, 14, 9, 4, 5, 10, 7, 15, 2, 11, 6, 13, 3, 8)
FIRST = 4
LATE = 4
MAX_GAP = 768

ridge_weight = 0.5


def make_table(seg_len, bins):
    sample_num = lax.iota(jnp.int32, seg_len)[:, None]
    bin_num = lax.iota(jnp.int32, bins)[None, :]
    angles = (sample_num * bin_num % seg_len).astype(jnp.float32) * (2.0 * math.pi / seg_len)
    hann_window = 0.5 - 0.5 * jnp.cos(sample_num.astype(jnp.float32) * (2.0 * math.pi / seg_len))
    return jnp.concatenate(
        [hann_window * jnp.cos(angles), -(hann_window * jnp.sin(angles))], axis=1
    ).astype(jnp.bfloat16)


def host_table(seg_len, bins):
    step = np.float32(2.0 * math.pi / seg_len)
    sample_num = np.arange(seg_len, dtype=np.int64)
    bin_num = np.arange(bins, dtype=np.int64)[:, None]
    angles = (sample_num[None, :] * bin_num % seg_len).astype(np.float32) * step
    hann_window = np.float32(0.5) - np.float32(0.5) * np.cos(sample_num.astype(np.float32) * step)
    return np.stack([hann_window * np.cos(angles), -(hann_window * np.sin(angles))]).astype(jnp.bfloat16)


def spectra_kernel(dest_of, count, starts_hbm, record_hbm, table_hbm, *rest):
    outs_hbm = rest[:-8]
    starts_ref, record_ref, table_ref, pieces_ref, out_ref, in_sem, table_sem, out_sem = rest[-8:]
    chans, samples = record_ref.shape
    dest_rows, seg_len = table_ref.shape[1:]
    segs = starts_ref.shape[0]
    wide = seg_len + LANES
    per_dot = 256 // chans
    per_block = min(count, 256 // dest_rows)
    starts_load = pltpu.make_async_copy(starts_hbm, starts_ref, in_sem.at[0])
    starts_load.start()
    ends = [min(samples, MAX_GAP * (first + per_dot - 1) + wide) for first in range(0, segs, per_dot)]
    loads, begin = [starts_load], 0
    for end in ends:
        if end > begin:
            part = pl.ds(begin, end - begin)
            loads.append(
                pltpu.make_async_copy(record_hbm.at[:, part], record_ref.at[:, part], in_sem.at[len(loads)])
            )
            begin = end
    loads += [
        pltpu.make_async_copy(table_hbm.at[dest_of(k)], table_ref.at[k], table_sem.at[k])
        for k in range(count)
    ]
    for load in loads[1:]:
        load.start()
    for load in loads:
        load.wait()
    lane = lax.broadcasted_iota(jnp.int32, (chans, LANES), 1)
    for seg in range(segs):
        start = starts_ref[seg]
        base = jnp.minimum(start // LANES * LANES, samples - wide)
        shift = start - base
        back = LANES - shift
        keep = lane < back
        here = pl.ds(seg * chans, chans)
        left = None
        for tile in range(seg_len // LANES + 1):
            at = pl.multiple_of(base + tile * LANES, LANES)
            right = pltpu.roll(
                record_ref[:, pl.ds(at, LANES)].astype(jnp.float32), lax.rem(back, LANES), 1
            )
            if tile:
                pieces_ref[here, pl.ds((tile - 1) * LANES, LANES)] = jnp.where(
                    keep, left, right
                ).astype(jnp.bfloat16)
            left = right
    stores = []
    for first_dest in range(0, count, per_block):
        held = min(per_block, count - first_dest)
        rows = pl.ds(first_dest * dest_rows, held * dest_rows)
        for first in range(0, segs, per_dot):
            cols = pl.ds(first * chans, per_dot * chans)
            out_ref[rows, cols] = lax.dot_general(
                table_ref[pl.ds(first_dest, held)].reshape(held * dest_rows, seg_len),
                pieces_ref[cols, :],
                (((1,), (1,)), ((), ())),
                preferred_element_type=jnp.float32,
            ).astype(jnp.bfloat16)
        for k in range(first_dest, first_dest + held):
            rows = pl.ds(k * dest_rows, dest_rows)
            to = outs_hbm[k] if len(outs_hbm) > 1 else outs_hbm[0].at[k]
            stores.append(pltpu.make_async_copy(out_ref.at[rows], to, out_sem.at[k]))
            stores[-1].start()
    for store in stores:
        store.wait()


def spectra_of(record, offsets, table, dest_of, count, apart):
    chans, samples = record.shape
    segs = offsets.shape[0]
    dest_rows, seg_len = table.shape[1:]
    cols = segs * chans
    if apart:
        out_shape = [jax.ShapeDtypeStruct((dest_rows, cols), jnp.bfloat16)] * count
    else:
        out_shape = [jax.ShapeDtypeStruct((count, dest_rows, cols), jnp.bfloat16)]
    return pl.pallas_call(
        functools.partial(spectra_kernel, dest_of, count),
        out_shape=out_shape,
        in_specs=[pl.BlockSpec(memory_space=pltpu.HBM)] * 3,
        out_specs=[pl.BlockSpec(memory_space=pltpu.HBM)] * len(out_shape),
        scratch_shapes=[
            pltpu.SMEM((segs,), jnp.int32),
            pltpu.VMEM((chans, samples), jnp.bfloat16),
            pltpu.VMEM((count, dest_rows, seg_len), jnp.bfloat16),
            pltpu.VMEM((cols, seg_len), jnp.bfloat16),
            pltpu.VMEM((count * dest_rows, cols), jnp.bfloat16),
            pltpu.SemaphoreType.DMA((cols // 256 + 1,)),
            pltpu.SemaphoreType.DMA((count,)),
            pltpu.SemaphoreType.DMA((count,)),
        ],
        compiler_params=pltpu.CompilerParams(vmem_limit_bytes=SPECTRA_LIMIT),
        cost_estimate=pl.CostEstimate(
            flops=2 * count * dest_rows * cols * seg_len,
            bytes_accessed=4 * count * dest_rows * cols,
            transcendentals=0,
        ),
        name="spectra",
    )(offsets, record, table)


def stacked(ref, group):
    tiles = ref.shape[1] // LANES
    rows = pl.ds(group * 2 * SUB, 2 * SUB)
    return jnp.concatenate([ref[rows, pl.ds(tile * LANES, LANES)] for tile in range(tiles)], axis=0)


def pick_kernel(shifts, index_ref, *rest):
    out_ref = rest[-1]
    chans = LANES // 2
    groups = out_ref.shape[0]
    index = index_ref[...]
    chan = lax.broadcasted_iota(jnp.int32, (LANES, LANES), 0)
    col = lax.broadcasted_iota(jnp.int32, (LANES, LANES), 1)
    same_seg = (chan >= chans) == (col >= chans)
    chan = jnp.where(chan >= chans, chan - chans, chan)
    if len(rest) > len(shifts) + 1:
        totals = [rest[-2][group].astype(jnp.float32) for group in range(groups)]
    else:
        totals = [jnp.zeros(out_ref.shape[1:], jnp.float32)] * groups
    for shift, ref in zip(shifts, rest):
        source = lax.axis_index("bin") ^ shift
        hit = same_seg & (chan + source * chans == index)
        pick = jnp.where(hit, 1.0, 0.0).astype(jnp.bfloat16)
        for group in range(groups):
            totals[group] = totals[group] + jnp.dot(
                stacked(ref, group), pick, preferred_element_type=jnp.float32
            )
    for group in range(groups):
        out_ref[group] = totals[group].astype(jnp.bfloat16)


def pick_refs(index, shifts, got, before):
    rows, cols = got[0].shape
    groups = rows // (2 * SUB)
    out_rows = cols // LANES * 2 * SUB
    operands = [index, *got] + ([] if before is None else [before])
    return pl.pallas_call(
        functools.partial(pick_kernel, shifts),
        out_shape=jax.ShapeDtypeStruct((groups, out_rows, LANES), jnp.bfloat16),
        in_specs=[pl.BlockSpec(memory_space=pltpu.VMEM)] * len(operands),
        out_specs=pl.BlockSpec(memory_space=pltpu.VMEM),
        compiler_params=pltpu.CompilerParams(vmem_limit_bytes=VMEM_LIMIT),
        cost_estimate=pl.CostEstimate(
            flops=2 * len(got) * groups * out_rows * LANES * LANES,
            bytes_accessed=2 * len(got) * rows * cols,
            transcendentals=0,
        ),
        name="pick_refs",
    )(*operands)


def turn_kernel(*refs):
    out_ref = refs[-1]
    chans = LANES // 2
    for at, ref in enumerate(refs[:-1]):
        here = pl.ds(at * chans, chans)
        for group in range(out_ref.shape[0]):
            turned = stacked(ref, group).T
            out_ref[group, here, 0:LANES] = turned[:chans]
            out_ref[group, here, LANES : 2 * LANES] = turned[chans:]


def turn(got):
    rows, cols = got[0].shape
    groups = rows // (2 * SUB)
    return pl.pallas_call(
        turn_kernel,
        out_shape=jax.ShapeDtypeStruct((groups, len(got) * LANES // 2, 2 * LANES), jnp.bfloat16),
        in_specs=[pl.BlockSpec(memory_space=pltpu.VMEM)] * len(got),
        out_specs=pl.BlockSpec(memory_space=pltpu.VMEM),
        compiler_params=pltpu.CompilerParams(vmem_limit_bytes=VMEM_LIMIT),
        cost_estimate=pl.CostEstimate(
            flops=0, bytes_accessed=4 * len(got) * rows * cols, transcendentals=0
        ),
        name="turn",
    )(*got)


def solve_steps(refs, segs, total_refs, found):
    wide = refs[0][0].shape
    spread = lambda x: jnp.broadcast_to(x, wide)
    real, imag = {}, {}
    for i in range(segs):
        for j in range(i + 1):
            (ir, ii), (jr, ji) = refs[i], refs[j]
            real[i, j] = spread(jnp.sum(ir * jr + ii * ji, axis=1, keepdims=True))
            if i != j:
                imag[i, j] = spread(jnp.sum(ir * ji - ii * jr, axis=1, keepdims=True))
            yield 6
    trace = real[0, 0]
    for i in range(1, segs):
        trace = trace + real[i, i]
    ridge = ridge_weight * trace / total_refs
    for i in range(segs):
        real[i, i] = real[i, i] + ridge
    yield 2 * segs
    right = [(r, -i) for r, i in refs]
    lower = {}
    inverse = []
    for k in range(segs):
        inv = 1.0 / real[k, k]
        inverse.append(inv)
        for i in range(k + 1, segs):
            lower[i, k] = (real[i, k] * inv, imag[i, k] * inv)
        yield 8 + 2 * (segs - k)
        for i in range(k + 1, segs):
            lr, li = lower[i, k]
            for j in range(k + 1, i):
                gr, gi = real[j, k], imag[j, k]
                real[i, j] = real[i, j] - (lr * gr + li * gi)
                imag[i, j] = imag[i, j] - (li * gr - lr * gi)
            real[i, i] = real[i, i] - (lr * real[i, k] + li * imag[i, k])
            br, bi = right[k]
            cr, ci = right[i]
            right[i] = (cr - (lr * br - li * bi), ci - (lr * bi + li * br))
            yield 8 * (i - k - 1) + 12
    for k in range(segs - 1, -1, -1):
        br, bi = right[k]
        vr, vi = br * inverse[k], bi * inverse[k]
        for i in range(k + 1, segs):
            lr, li = lower[i, k]
            wr, wi = found[i]
            vr = vr - (lr * wr + li * wi)
            vi = vi - (lr * wi - li * wr)
        found[k] = (vr, vi)
        yield 2 + 8 * (segs - 1 - k)


def solve_kernel(shifts, own_ref, other_ref, early_ref, late_ref, out_hbm, wide_ref, slot_ref, sem):
    half = LANES // 2
    groups, rows, _ = own_ref.shape
    chans = LANES // 2
    early, late = early_ref.shape[1], late_ref.shape[1]
    segs = 2 * rows // (2 * SUB)
    steps, pair = slot_ref.shape[:2]
    blocks = [(early_ref, at) for at in range(0, early, 256)] + [(late_ref, at) for at in range(0, late, 256)]
    sources = [lax.axis_index("bin") ^ shift for shift in shifts]
    first_half = lax.axis_index("grp") == 0
    row_bin = lax.broadcasted_iota(jnp.int32, wide_ref.shape[1:], 0) % SUB

    def copy_out(step, group):
        return pltpu.make_async_copy(
            slot_ref.at[step], out_hbm.at[pl.ds(group * SUB + step * pair, pair)], sem.at[step]
        )

    def solve(group, into):
        own = own_ref[group].astype(jnp.float32)
        other = other_ref[group].astype(jnp.float32)
        low = jnp.where(first_half, own, other)
        high = jnp.where(first_half, other, own)
        left = lax.broadcasted_iota(jnp.int32, low.shape, 1) < half
        even = jnp.where(left, low, pltpu.roll(high, half, 1))
        odd = jnp.where(left, pltpu.roll(low, half, 1), high)
        refs = []
        for seg in range(segs):
            source = odd if seg % 2 else even
            at = seg // 2 * 2 * SUB
            refs.append((source[at : at + SUB], source[at + SUB : at + 2 * SUB]))
        yield 100
        found = [None] * segs
        yield from solve_steps(refs, segs, LANES, found)
        for seg in range(segs):
            vr, vi = found[seg]
            at = (seg % 2) * LANES + seg // 2 * 2 * SUB
            wide_ref[into, at : at + SUB, 0:LANES] = vr
            wide_ref[into, at : at + SUB, LANES : 2 * LANES] = vi
            wide_ref[into, at + SUB : at + 2 * SUB, 0:LANES] = -vi
            wide_ref[into, at + SUB : at + 2 * SUB, LANES : 2 * LANES] = vr

    solve_cost = 100 + 6 * 136 + 32 + 8 * 16 + 240 + 8 * 560 + 12 * 120 + 32 + 960

    def apply(group, beside):
        done = 0
        for step in range(steps):
            if isinstance(group, int):
                copy_out(step, group).wait()
            else:

                @pl.when(group > 0)
                def _():
                    copy_out(step, group).wait()

            weights = jnp.concatenate(
                [
                    jnp.where(row_bin == step * pair + k, wide_ref[group % 2], 0.0).astype(jnp.bfloat16)
                    for k in range(pair)
                ],
                axis=1,
            )
            for block, (turned_ref, first) in enumerate(blocks):
                product = jnp.dot(
                    turned_ref[group, pl.ds(first, 256), :], weights, preferred_element_type=jnp.float32
                ).astype(jnp.bfloat16)
                for at in range(0, 256, chans):
                    source = sources[(block * 256 + at) // chans]
                    here = pl.ds(pl.multiple_of(source * chans, chans), chans)
                    for k in range(pair):
                        slot_ref[step, k, here, :] = product[
                            at : at + chans, k * 2 * LANES : (k + 1) * 2 * LANES
                        ]
                limit = solve_cost * (step * len(blocks) + block + 1) / (steps * len(blocks))
                while done < limit:
                    cost = next(beside, None)
                    if cost is None:
                        break
                    done += cost
            copy_out(step, group).start()
        for _ in beside:
            pass

    for _ in solve(0, 0):
        pass

    @pl.loop(0, groups - 1)
    def _(group):
        apply(group, solve(group + 1, (group + 1) % 2))

    apply(groups - 1, iter(()))
    for step in range(steps):
        copy_out(step, groups - 1).wait()


def solve_and_apply(shifts, own, other, early, late):
    groups, _, depth = early.shape
    chans = early.shape[1] + late.shape[1]
    pair = 2
    steps = SUB // pair
    return pl.pallas_call(
        functools.partial(solve_kernel, shifts),
        out_shape=jax.ShapeDtypeStruct((groups * SUB, chans, 2 * LANES), jnp.bfloat16),
        in_specs=[pl.BlockSpec(memory_space=pltpu.VMEM)] * 4,
        out_specs=pl.BlockSpec(memory_space=pltpu.HBM),
        scratch_shapes=[
            pltpu.VMEM((2, depth, 2 * LANES), jnp.float32),
            pltpu.VMEM((steps, pair, chans, 2 * LANES), jnp.bfloat16),
            pltpu.SemaphoreType.DMA((steps,)),
        ],
        compiler_params=pltpu.CompilerParams(vmem_limit_bytes=VMEM_LIMIT),
        cost_estimate=pl.CostEstimate(
            flops=2 * groups * SUB * chans * depth * 2 * LANES,
            bytes_accessed=groups * SUB * chans * 4 * LANES,
            transcendentals=0,
        ),
        name="solve_apply",
    )(own, other, early, late)


def local_kernels(record, ref_index, offsets):
    chan_rows = record[0]
    devices = lax.axis_size("bin")
    groups = NB // devices // SUB
    table = host_table(L, NB).reshape(2, devices, groups, SUB, L).transpose(1, 2, 0, 3, 4)
    table = jnp.asarray(table.reshape(devices, -1, L))
    index = jnp.concatenate([ref_index, ref_index], axis=1)
    me = lambda: lax.axis_index("bin")
    got = {}
    for part in (SHIFTS[:FIRST], SHIFTS[FIRST:] + (0,)):
        made = spectra_of(
            chan_rows, offsets, table, lambda k, part=part: me() ^ part[k], len(part), True
        )
        chan_rows, *made = lax.optimization_barrier((chan_rows, *made))
        for shift, block in zip(part, made):
            pairs = [(i, i ^ shift) for i in range(devices)]
            got[shift] = lax.ppermute(block, "bin", pairs) if shift else block
    early, late = (0,) + SHIFTS[:-LATE], SHIFTS[-LATE:]
    got_early, got_late = [got[shift] for shift in early], [got[shift] for shift in late]
    own = pick_refs(index, late, got_late, pick_refs(index, early, got_early, None))
    other = lax.ppermute(own, "grp", [(0, 1), (1, 0)])
    return solve_and_apply(early + late, own, other, turn(got_early), turn(got_late))


def transform(chan_rows, starts, dft_table, bin_devices):
    seg_len = dft_table.shape[0]
    pieces = jax.vmap(lambda start_at: lax.dynamic_slice_in_dim(chan_rows, start_at, seg_len, 1))(
        starts
    )
    spectra = jnp.einsum(
        "scn,nk->ksc", pieces, dft_table, preferred_element_type=jnp.float32
    ).astype(jnp.bfloat16)
    bin_total = dft_table.shape[1] // 2
    return spectra.reshape(
        2, bin_devices, bin_total // bin_devices, starts.shape[0], chan_rows.shape[0]
    )


def local(record, ref_index, offsets):
    chan_rows = record[0]
    dft_table = make_table(L, NB)
    bin_devices = lax.axis_size("bin")
    spectra = transform(chan_rows, offsets, dft_table, bin_devices)
    channels = lax.all_to_all(spectra, "bin", split_axis=1, concat_axis=4, tiled=True)[:, 0]
    local_refs = jnp.take(channels, ref_index[0], axis=3)
    references = lax.all_gather(local_refs, "grp", axis=3, tiled=True)
    ref_real = references[0]
    ref_imag = references[1]
    ref_blocks = jnp.stack(
        [
            jnp.concatenate([ref_real, -ref_imag], axis=-1),
            jnp.concatenate([ref_imag, ref_real], axis=-1),
        ]
    )
    bins_here = channels.shape[1]
    group_size = math.gcd(bins_here, 4)
    group_count = bins_here // group_size
    real_order = ref_blocks.shape[-1]

    def solve_bins(group_index):
        first_bin = group_index * group_size
        ref_group = lax.dynamic_slice_in_dim(ref_blocks, first_bin, group_size, 1)
        chan_group = lax.dynamic_slice_in_dim(channels, first_bin, group_size, 1)
        ref_rows = jnp.swapaxes(ref_group, 0, 1).reshape(group_size, -1, real_order)
        chan_cols = jnp.swapaxes(chan_group, 0, 1).reshape(group_size, -1, chan_group.shape[-1])
        gram_small = jnp.einsum(
            "fkr,fjr->fkj", ref_rows, ref_rows, preferred_element_type=jnp.float32
        )
        small_order = gram_small.shape[-1]
        ridge_term = ridge_weight * jnp.trace(gram_small, axis1=1, axis2=2) / real_order
        factor = jnp.linalg.cholesky(
            gram_small + ridge_term[:, None, None] * jnp.eye(small_order, dtype=jnp.float32)
        )
        solved = jax.scipy.linalg.cho_solve((factor, True), chan_cols.astype(jnp.float32))
        solved_high = solved.astype(jnp.bfloat16)
        solved_low = (solved - solved_high.astype(jnp.float32)).astype(jnp.bfloat16)
        transfer_t = jnp.einsum(
            "fkr,fkc->frc", ref_rows, solved_high, preferred_element_type=jnp.float32
        )
        transfer_t = transfer_t + jnp.einsum(
            "fkr,fkc->frc", ref_rows, solved_low, preferred_element_type=jnp.float32
        )
        return jnp.swapaxes(transfer_t, 1, 2).astype(jnp.bfloat16)

    results = lax.map(solve_bins, jnp.arange(group_count))
    return results.reshape(bins_here, results.shape[2], results.shape[3])


def solution(mesh):
    placed = (P("grp", "bin", None), P("grp", None), P())
    devices, groups = mesh.shape["bin"], mesh.shape["grp"]

    def whole(record, ref_index, offsets):
        chans = record.shape[1] // devices
        kernels = (
            devices == 1 + len(SHIFTS)
            and groups == 2
            and 2 * chans == LANES
            and groups * ref_index.shape[1] == LANES
            and offsets.shape[0] == 2 * SUB
            and NB // devices % SUB == 0
            and NB // devices >= 2 * SUB
        )
        return jax.shard_map(
            local_kernels if kernels else local,
            mesh=mesh,
            in_specs=placed,
            out_specs=P("bin", "grp", None),
            check_vma=False,
        )(record, ref_index, offsets)

    return whole
```

```python
import functools
import math

import jax
import jax.numpy as jnp
import numpy as np
from jax import lax
from jax.experimental import pallas as pl
from jax.experimental.pallas import tpu as pltpu
from jax.sharding import PartitionSpec as P

L = 1024
NB = 512
LANES = 128
SUB = 8
VMEM_LIMIT = 48 * 1024 * 1024
SPECTRA_LIMIT = 66000000
SHIFTS = (12, 1, 14, 9, 4, 5, 10, 7, 15, 2, 11, 6, 13, 3, 8)
FIRST = 4
SECOND = 8
LATE = 4
MAX_GAP = 768

ridge_weight = 0.5


def make_table(seg_len, bins):
    sample_num = lax.iota(jnp.int32, seg_len)[:, None]
    bin_num = lax.iota(jnp.int32, bins)[None, :]
    angles = (sample_num * bin_num % seg_len).astype(jnp.float32) * (2.0 * math.pi / seg_len)
    hann_window = 0.5 - 0.5 * jnp.cos(sample_num.astype(jnp.float32) * (2.0 * math.pi / seg_len))
    return jnp.concatenate(
        [hann_window * jnp.cos(angles), -(hann_window * jnp.sin(angles))], axis=1
    ).astype(jnp.bfloat16)


def host_table(seg_len, bins):
    step = np.float32(2.0 * math.pi / seg_len)
    sample_num = np.arange(seg_len, dtype=np.int64)
    bin_num = np.arange(bins, dtype=np.int64)[:, None]
    angles = (sample_num[None, :] * bin_num % seg_len).astype(np.float32) * step
    hann_window = np.float32(0.5) - np.float32(0.5) * np.cos(sample_num.astype(np.float32) * step)
    return np.stack([hann_window * np.cos(angles), -(hann_window * np.sin(angles))]).astype(jnp.bfloat16)


def spectra_kernel(dest_of, count, starts_hbm, record_hbm, table_hbm, *rest):
    outs_hbm = rest[:-8]
    starts_ref, record_ref, table_ref, pieces_ref, out_ref, in_sem, table_sem, out_sem = rest[-8:]
    chans, samples = record_ref.shape
    dest_rows, seg_len = table_ref.shape[1:]
    segs = starts_ref.shape[0]
    wide = seg_len + LANES
    per_dot = 256 // chans
    per_block = min(count, 256 // dest_rows)
    starts_load = pltpu.make_async_copy(starts_hbm, starts_ref, in_sem.at[0])
    starts_load.start()
    ends = [min(samples, MAX_GAP * (first + per_dot - 1) + wide) for first in range(0, segs, per_dot)]
    loads, begin = [starts_load], 0
    for end in ends:
        if end > begin:
            part = pl.ds(begin, end - begin)
            loads.append(
                pltpu.make_async_copy(record_hbm.at[:, part], record_ref.at[:, part], in_sem.at[len(loads)])
            )
            begin = end
    loads += [
        pltpu.make_async_copy(table_hbm.at[dest_of(k)], table_ref.at[k], table_sem.at[k])
        for k in range(count)
    ]
    for load in loads[1:]:
        load.start()
    for load in loads:
        load.wait()
    lane = lax.broadcasted_iota(jnp.int32, (chans, LANES), 1)
    for seg in range(segs):
        start = starts_ref[seg]
        base = jnp.minimum(start // LANES * LANES, samples - wide)
        shift = start - base
        back = LANES - shift
        keep = lane < back
        here = pl.ds(seg * chans, chans)
        left = None
        for tile in range(seg_len // LANES + 1):
            at = pl.multiple_of(base + tile * LANES, LANES)
            right = pltpu.roll(
                record_ref[:, pl.ds(at, LANES)].astype(jnp.float32), lax.rem(back, LANES), 1
            )
            if tile:
                pieces_ref[here, pl.ds((tile - 1) * LANES, LANES)] = jnp.where(
                    keep, left, right
                ).astype(jnp.bfloat16)
            left = right
    stores = []
    for first_dest in range(0, count, per_block):
        held = min(per_block, count - first_dest)
        rows = pl.ds(first_dest * dest_rows, held * dest_rows)
        for first in range(0, segs, per_dot):
            cols = pl.ds(first * chans, per_dot * chans)
            out_ref[rows, cols] = lax.dot_general(
                table_ref[pl.ds(first_dest, held)].reshape(held * dest_rows, seg_len),
                pieces_ref[cols, :],
                (((1,), (1,)), ((), ())),
                preferred_element_type=jnp.float32,
            ).astype(jnp.bfloat16)
        for k in range(first_dest, first_dest + held):
            rows = pl.ds(k * dest_rows, dest_rows)
            to = outs_hbm[k] if len(outs_hbm) > 1 else outs_hbm[0].at[k]
            stores.append(pltpu.make_async_copy(out_ref.at[rows], to, out_sem.at[k]))
            stores[-1].start()
    for store in stores:
        store.wait()


def spectra_of(record, offsets, table, dest_of, count, apart):
    chans, samples = record.shape
    segs = offsets.shape[0]
    dest_rows, seg_len = table.shape[1:]
    cols = segs * chans
    if apart:
        out_shape = [jax.ShapeDtypeStruct((dest_rows, cols), jnp.bfloat16)] * count
    else:
        out_shape = [jax.ShapeDtypeStruct((count, dest_rows, cols), jnp.bfloat16)]
    return pl.pallas_call(
        functools.partial(spectra_kernel, dest_of, count),
        out_shape=out_shape,
        in_specs=[pl.BlockSpec(memory_space=pltpu.HBM)] * 3,
        out_specs=[pl.BlockSpec(memory_space=pltpu.HBM)] * len(out_shape),
        scratch_shapes=[
            pltpu.SMEM((segs,), jnp.int32),
            pltpu.VMEM((chans, samples), jnp.bfloat16),
            pltpu.VMEM((count, dest_rows, seg_len), jnp.bfloat16),
            pltpu.VMEM((cols, seg_len), jnp.bfloat16),
            pltpu.VMEM((count * dest_rows, cols), jnp.bfloat16),
            pltpu.SemaphoreType.DMA((cols // 256 + 1,)),
            pltpu.SemaphoreType.DMA((count,)),
            pltpu.SemaphoreType.DMA((count,)),
        ],
        compiler_params=pltpu.CompilerParams(vmem_limit_bytes=SPECTRA_LIMIT),
        cost_estimate=pl.CostEstimate(
            flops=2 * count * dest_rows * cols * seg_len,
            bytes_accessed=4 * count * dest_rows * cols,
            transcendentals=0,
        ),
        name="spectra",
    )(offsets, record, table)


def stacked(ref, group):
    tiles = ref.shape[1] // LANES
    rows = pl.ds(group * 2 * SUB, 2 * SUB)
    return jnp.concatenate([ref[rows, pl.ds(tile * LANES, LANES)] for tile in range(tiles)], axis=0)


def pick_kernel(shifts, index_ref, *rest):
    out_ref = rest[-1]
    chans = LANES // 2
    groups = out_ref.shape[0]
    index = index_ref[...]
    chan = lax.broadcasted_iota(jnp.int32, (LANES, LANES), 0)
    col = lax.broadcasted_iota(jnp.int32, (LANES, LANES), 1)
    same_seg = (chan >= chans) == (col >= chans)
    chan = jnp.where(chan >= chans, chan - chans, chan)
    if len(rest) > len(shifts) + 1:
        totals = [rest[-2][group].astype(jnp.float32) for group in range(groups)]
    else:
        totals = [jnp.zeros(out_ref.shape[1:], jnp.float32)] * groups
    for shift, ref in zip(shifts, rest):
        source = lax.axis_index("bin") ^ shift
        hit = same_seg & (chan + source * chans == index)
        pick = jnp.where(hit, 1.0, 0.0).astype(jnp.bfloat16)
        for group in range(groups):
            totals[group] = totals[group] + jnp.dot(
                stacked(ref, group), pick, preferred_element_type=jnp.float32
            )
    for group in range(groups):
        out_ref[group] = totals[group].astype(jnp.bfloat16)


def pick_refs(index, shifts, got, before):
    rows, cols = got[0].shape
    groups = rows // (2 * SUB)
    out_rows = cols // LANES * 2 * SUB
    operands = [index, *got] + ([] if before is None else [before])
    return pl.pallas_call(
        functools.partial(pick_kernel, shifts),
        out_shape=jax.ShapeDtypeStruct((groups, out_rows, LANES), jnp.bfloat16),
        in_specs=[pl.BlockSpec(memory_space=pltpu.VMEM)] * len(operands),
        out_specs=pl.BlockSpec(memory_space=pltpu.VMEM),
        compiler_params=pltpu.CompilerParams(vmem_limit_bytes=VMEM_LIMIT),
        cost_estimate=pl.CostEstimate(
            flops=2 * len(got) * groups * out_rows * LANES * LANES,
            bytes_accessed=2 * len(got) * rows * cols,
            transcendentals=0,
        ),
        name="pick_refs",
    )(*operands)


def turn_kernel(*refs):
    out_ref = refs[-1]
    chans = LANES // 2
    for at, ref in enumerate(refs[:-1]):
        here = pl.ds(at * chans, chans)
        for group in range(out_ref.shape[0]):
            turned = stacked(ref, group).T
            out_ref[group, here, 0:LANES] = turned[:chans]
            out_ref[group, here, LANES : 2 * LANES] = turned[chans:]


def turn(got):
    rows, cols = got[0].shape
    groups = rows // (2 * SUB)
    return pl.pallas_call(
        turn_kernel,
        out_shape=jax.ShapeDtypeStruct((groups, len(got) * LANES // 2, 2 * LANES), jnp.bfloat16),
        in_specs=[pl.BlockSpec(memory_space=pltpu.VMEM)] * len(got),
        out_specs=pl.BlockSpec(memory_space=pltpu.VMEM),
        compiler_params=pltpu.CompilerParams(vmem_limit_bytes=VMEM_LIMIT),
        cost_estimate=pl.CostEstimate(
            flops=0, bytes_accessed=4 * len(got) * rows * cols, transcendentals=0
        ),
        name="turn",
    )(*got)


def solve_steps(refs, segs, total_refs, found):
    wide = refs[0][0].shape
    spread = lambda x: jnp.broadcast_to(x, wide)
    real, imag = {}, {}
    for i in range(segs):
        for j in range(i + 1):
            (ir, ii), (jr, ji) = refs[i], refs[j]
            real[i, j] = spread(jnp.sum(ir * jr + ii * ji, axis=1, keepdims=True))
            if i != j:
                imag[i, j] = spread(jnp.sum(ir * ji - ii * jr, axis=1, keepdims=True))
            yield 6
    trace = real[0, 0]
    for i in range(1, segs):
        trace = trace + real[i, i]
    ridge = ridge_weight * trace / total_refs
    for i in range(segs):
        real[i, i] = real[i, i] + ridge
    yield 2 * segs
    right = [(r, -i) for r, i in refs]
    lower = {}
    inverse = []
    for k in range(segs):
        inv = 1.0 / real[k, k]
        inverse.append(inv)
        for i in range(k + 1, segs):
            lower[i, k] = (real[i, k] * inv, imag[i, k] * inv)
        yield 8 + 2 * (segs - k)
        for i in range(k + 1, segs):
            lr, li = lower[i, k]
            for j in range(k + 1, i):
                gr, gi = real[j, k], imag[j, k]
                real[i, j] = real[i, j] - (lr * gr + li * gi)
                imag[i, j] = imag[i, j] - (li * gr - lr * gi)
            real[i, i] = real[i, i] - (lr * real[i, k] + li * imag[i, k])
            br, bi = right[k]
            cr, ci = right[i]
            right[i] = (cr - (lr * br - li * bi), ci - (lr * bi + li * br))
            yield 8 * (i - k - 1) + 12
    for k in range(segs - 1, -1, -1):
        br, bi = right[k]
        vr, vi = br * inverse[k], bi * inverse[k]
        for i in range(k + 1, segs):
            lr, li = lower[i, k]
            wr, wi = found[i]
            vr = vr - (lr * wr + li * wi)
            vi = vi - (lr * wi - li * wr)
        found[k] = (vr, vi)
        yield 2 + 8 * (segs - 1 - k)


def solve_kernel(shifts, own_ref, other_ref, early_ref, late_ref, out_hbm, wide_ref, slot_ref, sem):
    half = LANES // 2
    groups, rows, _ = own_ref.shape
    chans = LANES // 2
    early, late = early_ref.shape[1], late_ref.shape[1]
    segs = 2 * rows // (2 * SUB)
    steps, pair = slot_ref.shape[:2]
    blocks = [(early_ref, at) for at in range(0, early, 256)] + [(late_ref, at) for at in range(0, late, 256)]
    sources = [lax.axis_index("bin") ^ shift for shift in shifts]
    first_half = lax.axis_index("grp") == 0
    row_bin = lax.broadcasted_iota(jnp.int32, (2 * SUB, 2 * LANES), 0) % SUB

    def copy_out(step, group):
        return pltpu.make_async_copy(
            slot_ref.at[step], out_hbm.at[pl.ds(group * SUB + step * pair, pair)], sem.at[step]
        )

    def solve(group, into):
        own = own_ref[group].astype(jnp.float32)
        other = other_ref[group].astype(jnp.float32)
        low = jnp.where(first_half, own, other)
        high = jnp.where(first_half, other, own)
        left = lax.broadcasted_iota(jnp.int32, low.shape, 1) < half
        even = jnp.where(left, low, pltpu.roll(high, half, 1))
        odd = jnp.where(left, pltpu.roll(low, half, 1), high)
        refs = []
        for seg in range(segs):
            source = odd if seg % 2 else even
            at = seg // 2 * 2 * SUB
            refs.append((source[at : at + SUB], source[at + SUB : at + 2 * SUB]))
        yield 100
        found = [None] * segs
        yield from solve_steps(refs, segs, LANES, found)
        for seg in range(segs):
            vr, vi = found[seg]
            at = (seg % 2) * LANES + seg // 2 * 2 * SUB
            here = pl.ds(at, 2 * SUB)
            wide_ref[into, here, 0:LANES] = jnp.concatenate([vr, -vi], axis=0).astype(jnp.bfloat16)
            wide_ref[into, here, LANES : 2 * LANES] = jnp.concatenate([vi, vr], axis=0).astype(
                jnp.bfloat16
            )

    solve_cost = 100 + 6 * 136 + 32 + 8 * 16 + 240 + 8 * 560 + 12 * 120 + 32 + 960

    def apply(group, beside):
        done = 0
        for step in range(steps):
            if isinstance(group, int):
                copy_out(step, group).wait()
            else:

                @pl.when(group > 0)
                def _():
                    copy_out(step, group).wait()

            tiles = wide_ref[group % 2].reshape(-1, 2 * SUB, 2 * LANES)
            weights = jnp.concatenate(
                [
                    jnp.where(
                        (row_bin == step * pair + k)[None], tiles, jnp.zeros_like(tiles)
                    ).reshape(wide_ref.shape[1:])
                    for k in range(pair)
                ],
                axis=1,
            )
            for block, (turned_ref, first) in enumerate(blocks):
                product = jnp.dot(
                    turned_ref[group, pl.ds(first, 256), :], weights, preferred_element_type=jnp.float32
                ).astype(jnp.bfloat16)
                for at in range(0, 256, chans):
                    source = sources[(block * 256 + at) // chans]
                    here = pl.ds(pl.multiple_of(source * chans, chans), chans)
                    for k in range(pair):
                        slot_ref[step, k, here, :] = product[
                            at : at + chans, k * 2 * LANES : (k + 1) * 2 * LANES
                        ]
                limit = solve_cost * (step * len(blocks) + block + 1) / (steps * len(blocks))
                while done < limit:
                    cost = next(beside, None)
                    if cost is None:
                        break
                    done += cost
            copy_out(step, group).start()
        for _ in beside:
            pass

    for _ in solve(0, 0):
        pass

    @pl.loop(0, groups - 1)
    def _(group):
        apply(group, solve(group + 1, (group + 1) % 2))

    apply(groups - 1, iter(()))
    for step in range(steps):
        copy_out(step, groups - 1).wait()


def solve_and_apply(shifts, own, other, early, late):
    groups, _, depth = early.shape
    chans = early.shape[1] + late.shape[1]
    pair = 2
    steps = SUB // pair
    return pl.pallas_call(
        functools.partial(solve_kernel, shifts),
        out_shape=jax.ShapeDtypeStruct((groups * SUB, chans, 2 * LANES), jnp.bfloat16),
        in_specs=[pl.BlockSpec(memory_space=pltpu.VMEM)] * 4,
        out_specs=pl.BlockSpec(memory_space=pltpu.HBM),
        scratch_shapes=[
            pltpu.VMEM((2, depth, 2 * LANES), jnp.bfloat16),
            pltpu.VMEM((steps, pair, chans, 2 * LANES), jnp.bfloat16),
            pltpu.SemaphoreType.DMA((steps,)),
        ],
        compiler_params=pltpu.CompilerParams(vmem_limit_bytes=VMEM_LIMIT),
        cost_estimate=pl.CostEstimate(
            flops=2 * groups * SUB * chans * depth * 2 * LANES,
            bytes_accessed=groups * SUB * chans * 4 * LANES,
            transcendentals=0,
        ),
        name="solve_apply",
    )(own, other, early, late)


def local_kernels(record, ref_index, offsets):
    chan_rows = record[0]
    devices = lax.axis_size("bin")
    groups = NB // devices // SUB
    table = host_table(L, NB).reshape(2, devices, groups, SUB, L).transpose(1, 2, 0, 3, 4)
    table = jnp.asarray(table.reshape(devices, -1, L))
    index = jnp.concatenate([ref_index, ref_index], axis=1)
    me = lambda: lax.axis_index("bin")
    got = {}
    for part in (SHIFTS[:FIRST], SHIFTS[FIRST:SECOND], SHIFTS[SECOND:] + (0,)):
        made = spectra_of(
            chan_rows, offsets, table, lambda k, part=part: me() ^ part[k], len(part), True
        )
        chan_rows, *made = lax.optimization_barrier((chan_rows, *made))
        for shift, block in zip(part, made):
            pairs = [(i, i ^ shift) for i in range(devices)]
            got[shift] = lax.ppermute(block, "bin", pairs) if shift else block
    early, late = (0,) + SHIFTS[:-LATE], SHIFTS[-LATE:]
    got_early, got_late = [got[shift] for shift in early], [got[shift] for shift in late]
    own = pick_refs(index, late, got_late, pick_refs(index, early, got_early, None))
    other = lax.ppermute(own, "grp", [(0, 1), (1, 0)])
    return solve_and_apply(early + late, own, other, turn(got_early), turn(got_late))


def transform(chan_rows, starts, dft_table, bin_devices):
    seg_len = dft_table.shape[0]
    pieces = jax.vmap(lambda start_at: lax.dynamic_slice_in_dim(chan_rows, start_at, seg_len, 1))(
        starts
    )
    spectra = jnp.einsum(
        "scn,nk->ksc", pieces, dft_table, preferred_element_type=jnp.float32
    ).astype(jnp.bfloat16)
    bin_total = dft_table.shape[1] // 2
    return spectra.reshape(
        2, bin_devices, bin_total // bin_devices, starts.shape[0], chan_rows.shape[0]
    )


def local(record, ref_index, offsets):
    chan_rows = record[0]
    dft_table = make_table(L, NB)
    bin_devices = lax.axis_size("bin")
    spectra = transform(chan_rows, offsets, dft_table, bin_devices)
    channels = lax.all_to_all(spectra, "bin", split_axis=1, concat_axis=4, tiled=True)[:, 0]
    local_refs = jnp.take(channels, ref_index[0], axis=3)
    references = lax.all_gather(local_refs, "grp", axis=3, tiled=True)
    ref_real = references[0]
    ref_imag = references[1]
    ref_blocks = jnp.stack(
        [
            jnp.concatenate([ref_real, -ref_imag], axis=-1),
            jnp.concatenate([ref_imag, ref_real], axis=-1),
        ]
    )
    bins_here = channels.shape[1]
    group_size = math.gcd(bins_here, 4)
    group_count = bins_here // group_size
    real_order = ref_blocks.shape[-1]

    def solve_bins(group_index):
        first_bin = group_index * group_size
        ref_group = lax.dynamic_slice_in_dim(ref_blocks, first_bin, group_size, 1)
        chan_group = lax.dynamic_slice_in_dim(channels, first_bin, group_size, 1)
        ref_rows = jnp.swapaxes(ref_group, 0, 1).reshape(group_size, -1, real_order)
        chan_cols = jnp.swapaxes(chan_group, 0, 1).reshape(group_size, -1, chan_group.shape[-1])
        gram_small = jnp.einsum(
            "fkr,fjr->fkj", ref_rows, ref_rows, preferred_element_type=jnp.float32
        )
        small_order = gram_small.shape[-1]
        ridge_term = ridge_weight * jnp.trace(gram_small, axis1=1, axis2=2) / real_order
        factor = jnp.linalg.cholesky(
            gram_small + ridge_term[:, None, None] * jnp.eye(small_order, dtype=jnp.float32)
        )
        solved = jax.scipy.linalg.cho_solve((factor, True), chan_cols.astype(jnp.float32))
        solved_high = solved.astype(jnp.bfloat16)
        solved_low = (solved - solved_high.astype(jnp.float32)).astype(jnp.bfloat16)
        transfer_t = jnp.einsum(
            "fkr,fkc->frc", ref_rows, solved_high, preferred_element_type=jnp.float32
        )
        transfer_t = transfer_t + jnp.einsum(
            "fkr,fkc->frc", ref_rows, solved_low, preferred_element_type=jnp.float32
        )
        return jnp.swapaxes(transfer_t, 1, 2).astype(jnp.bfloat16)

    results = lax.map(solve_bins, jnp.arange(group_count))
    return results.reshape(bins_here, results.shape[2], results.shape[3])


def solution(mesh):
    placed = (P("grp", "bin", None), P("grp", None), P())
    devices, groups = mesh.shape["bin"], mesh.shape["grp"]

    def whole(record, ref_index, offsets):
        chans = record.shape[1] // devices
        kernels = (
            devices == 1 + len(SHIFTS)
            and groups == 2
            and 2 * chans == LANES
            and groups * ref_index.shape[1] == LANES
            and offsets.shape[0] == 2 * SUB
            and NB // devices % SUB == 0
            and NB // devices >= 2 * SUB
        )
        return jax.shard_map(
            local_kernels if kernels else local,
            mesh=mesh,
            in_specs=placed,
            out_specs=P("bin", "grp", None),
            check_vma=False,
        )(record, ref_index, offsets)

    return whole
```

```python
import functools
import math

import jax
import jax.numpy as jnp
import numpy as np
from jax import lax
from jax.experimental import pallas as pl
from jax.experimental.pallas import tpu as pltpu
from jax.sharding import PartitionSpec as P

L = 1024
NB = 512
LANES = 128
SUB = 8
VMEM_LIMIT = 48 * 1024 * 1024
SPECTRA_LIMIT = 66000000
SHIFTS = (12, 1, 14, 9, 4, 5, 10, 7, 15, 2, 11, 6, 13, 3, 8)
FIRST = 4
LATE = 4
MAX_GAP = 768

ridge_weight = 0.5


def make_table(seg_len, bins):
    sample_num = lax.iota(jnp.int32, seg_len)[:, None]
    bin_num = lax.iota(jnp.int32, bins)[None, :]
    angles = (sample_num * bin_num % seg_len).astype(jnp.float32) * (2.0 * math.pi / seg_len)
    hann_window = 0.5 - 0.5 * jnp.cos(sample_num.astype(jnp.float32) * (2.0 * math.pi / seg_len))
    return jnp.concatenate(
        [hann_window * jnp.cos(angles), -(hann_window * jnp.sin(angles))], axis=1
    ).astype(jnp.bfloat16)


def host_table(seg_len, bins):
    step = np.float32(2.0 * math.pi / seg_len)
    sample_num = np.arange(seg_len, dtype=np.int64)
    bin_num = np.arange(bins, dtype=np.int64)[:, None]
    angles = (sample_num[None, :] * bin_num % seg_len).astype(np.float32) * step
    hann_window = np.float32(0.5) - np.float32(0.5) * np.cos(sample_num.astype(np.float32) * step)
    return np.stack([hann_window * np.cos(angles), -(hann_window * np.sin(angles))]).astype(jnp.bfloat16)


def spectra_kernel(dest_of, count, starts_hbm, record_hbm, table_hbm, *rest):
    outs_hbm = rest[:-8]
    starts_ref, record_ref, table_ref, pieces_ref, out_ref, in_sem, table_sem, out_sem = rest[-8:]
    chans, samples = record_ref.shape
    dest_rows, seg_len = table_ref.shape[1:]
    segs = starts_ref.shape[0]
    wide = seg_len + LANES
    per_dot = 256 // chans
    per_block = min(count, 256 // dest_rows)
    starts_load = pltpu.make_async_copy(starts_hbm, starts_ref, in_sem.at[0])
    starts_load.start()
    ends = [min(samples, MAX_GAP * (first + per_dot - 1) + wide) for first in range(0, segs, per_dot)]
    loads, begin = [starts_load], 0
    for end in ends:
        if end > begin:
            part = pl.ds(begin, end - begin)
            loads.append(
                pltpu.make_async_copy(record_hbm.at[:, part], record_ref.at[:, part], in_sem.at[len(loads)])
            )
            begin = end
    loads += [
        pltpu.make_async_copy(table_hbm.at[dest_of(k)], table_ref.at[k], table_sem.at[k])
        for k in range(count)
    ]
    for load in loads[1:]:
        load.start()
    for load in loads:
        load.wait()
    lane = lax.broadcasted_iota(jnp.int32, (chans, LANES), 1)
    for seg in range(segs):
        start = starts_ref[seg]
        base = jnp.minimum(start // LANES * LANES, samples - wide)
        shift = start - base
        back = LANES - shift
        keep = lane < back
        here = pl.ds(seg * chans, chans)
        left = None
        for tile in range(seg_len // LANES + 1):
            at = pl.multiple_of(base + tile * LANES, LANES)
            right = pltpu.roll(
                record_ref[:, pl.ds(at, LANES)].astype(jnp.float32), lax.rem(back, LANES), 1
            )
            if tile:
                pieces_ref[here, pl.ds((tile - 1) * LANES, LANES)] = jnp.where(
                    keep, left, right
                ).astype(jnp.bfloat16)
            left = right
    stores = []
    for first_dest in range(0, count, per_block):
        held = min(per_block, count - first_dest)
        rows = pl.ds(first_dest * dest_rows, held * dest_rows)
        for first in range(0, segs, per_dot):
            cols = pl.ds(first * chans, per_dot * chans)
            out_ref[rows, cols] = lax.dot_general(
                table_ref[pl.ds(first_dest, held)].reshape(held * dest_rows, seg_len),
                pieces_ref[cols, :],
                (((1,), (1,)), ((), ())),
                preferred_element_type=jnp.float32,
            ).astype(jnp.bfloat16)
        for k in range(first_dest, first_dest + held):
            rows = pl.ds(k * dest_rows, dest_rows)
            to = outs_hbm[k] if len(outs_hbm) > 1 else outs_hbm[0].at[k]
            stores.append(pltpu.make_async_copy(out_ref.at[rows], to, out_sem.at[k]))
            stores[-1].start()
    for store in stores:
        store.wait()


def spectra_of(record, offsets, table, dest_of, count, apart):
    chans, samples = record.shape
    segs = offsets.shape[0]
    dest_rows, seg_len = table.shape[1:]
    cols = segs * chans
    if apart:
        out_shape = [jax.ShapeDtypeStruct((dest_rows, cols), jnp.bfloat16)] * count
    else:
        out_shape = [jax.ShapeDtypeStruct((count, dest_rows, cols), jnp.bfloat16)]
    return pl.pallas_call(
        functools.partial(spectra_kernel, dest_of, count),
        out_shape=out_shape,
        in_specs=[pl.BlockSpec(memory_space=pltpu.HBM)] * 3,
        out_specs=[pl.BlockSpec(memory_space=pltpu.HBM)] * len(out_shape),
        scratch_shapes=[
            pltpu.SMEM((segs,), jnp.int32),
            pltpu.VMEM((chans, samples), jnp.bfloat16),
            pltpu.VMEM((count, dest_rows, seg_len), jnp.bfloat16),
            pltpu.VMEM((cols, seg_len), jnp.bfloat16),
            pltpu.VMEM((count * dest_rows, cols), jnp.bfloat16),
            pltpu.SemaphoreType.DMA((cols // 256 + 1,)),
            pltpu.SemaphoreType.DMA((count,)),
            pltpu.SemaphoreType.DMA((count,)),
        ],
        compiler_params=pltpu.CompilerParams(vmem_limit_bytes=SPECTRA_LIMIT),
        cost_estimate=pl.CostEstimate(
            flops=2 * count * dest_rows * cols * seg_len,
            bytes_accessed=4 * count * dest_rows * cols,
            transcendentals=0,
        ),
        name="spectra",
    )(offsets, record, table)


def stacked(ref, group):
    tiles = ref.shape[1] // LANES
    rows = pl.ds(group * 2 * SUB, 2 * SUB)
    return jnp.concatenate([ref[rows, pl.ds(tile * LANES, LANES)] for tile in range(tiles)], axis=0)


def pick_kernel(shifts, index_ref, *rest):
    out_ref = rest[-1]
    chans = LANES // 2
    groups = out_ref.shape[0]
    index = index_ref[...]
    chan = lax.broadcasted_iota(jnp.int32, (LANES, LANES), 0)
    col = lax.broadcasted_iota(jnp.int32, (LANES, LANES), 1)
    same_seg = (chan >= chans) == (col >= chans)
    chan = jnp.where(chan >= chans, chan - chans, chan)
    if len(rest) > len(shifts) + 1:
        totals = [rest[-2][group].astype(jnp.float32) for group in range(groups)]
    else:
        totals = [jnp.zeros(out_ref.shape[1:], jnp.float32)] * groups
    for shift, ref in zip(shifts, rest):
        source = lax.axis_index("bin") ^ shift
        hit = same_seg & (chan + source * chans == index)
        pick = jnp.where(hit, 1.0, 0.0).astype(jnp.bfloat16)
        for group in range(groups):
            totals[group] = totals[group] + jnp.dot(
                stacked(ref, group), pick, preferred_element_type=jnp.float32
            )
    for group in range(groups):
        out_ref[group] = totals[group].astype(jnp.bfloat16)


def pick_refs(index, shifts, got, before):
    rows, cols = got[0].shape
    groups = rows // (2 * SUB)
    out_rows = cols // LANES * 2 * SUB
    operands = [index, *got] + ([] if before is None else [before])
    return pl.pallas_call(
        functools.partial(pick_kernel, shifts),
        out_shape=jax.ShapeDtypeStruct((groups, out_rows, LANES), jnp.bfloat16),
        in_specs=[pl.BlockSpec(memory_space=pltpu.VMEM)] * len(operands),
        out_specs=pl.BlockSpec(memory_space=pltpu.VMEM),
        compiler_params=pltpu.CompilerParams(vmem_limit_bytes=VMEM_LIMIT),
        cost_estimate=pl.CostEstimate(
            flops=2 * len(got) * groups * out_rows * LANES * LANES,
            bytes_accessed=2 * len(got) * rows * cols,
            transcendentals=0,
        ),
        name="pick_refs",
    )(*operands)


def turn_kernel(*refs):
    out_ref = refs[-1]
    chans = LANES // 2
    for at, ref in enumerate(refs[:-1]):
        here = pl.ds(at * chans, chans)
        for group in range(out_ref.shape[0]):
            turned = stacked(ref, group).T
            out_ref[group, here, 0:LANES] = turned[:chans]
            out_ref[group, here, LANES : 2 * LANES] = turned[chans:]


def turn(got):
    rows, cols = got[0].shape
    groups = rows // (2 * SUB)
    return pl.pallas_call(
        turn_kernel,
        out_shape=jax.ShapeDtypeStruct((groups, len(got) * LANES // 2, 2 * LANES), jnp.bfloat16),
        in_specs=[pl.BlockSpec(memory_space=pltpu.VMEM)] * len(got),
        out_specs=pl.BlockSpec(memory_space=pltpu.VMEM),
        compiler_params=pltpu.CompilerParams(vmem_limit_bytes=VMEM_LIMIT),
        cost_estimate=pl.CostEstimate(
            flops=0, bytes_accessed=4 * len(got) * rows * cols, transcendentals=0
        ),
        name="turn",
    )(*got)


def solve_steps(refs, segs, total_refs, found):
    wide = refs[0][0].shape
    spread = lambda x: jnp.broadcast_to(x, wide)
    real, imag = {}, {}
    for i in range(segs):
        for j in range(i + 1):
            (ir, ii), (jr, ji) = refs[i], refs[j]
            real[i, j] = spread(jnp.sum(ir * jr + ii * ji, axis=1, keepdims=True))
            if i != j:
                imag[i, j] = spread(jnp.sum(ir * ji - ii * jr, axis=1, keepdims=True))
            yield 6
    trace = real[0, 0]
    for i in range(1, segs):
        trace = trace + real[i, i]
    ridge = ridge_weight * trace / total_refs
    for i in range(segs):
        real[i, i] = real[i, i] + ridge
    yield 2 * segs
    right = [(r, -i) for r, i in refs]
    lower = {}
    inverse = []
    for k in range(segs):
        inv = 1.0 / real[k, k]
        inverse.append(inv)
        for i in range(k + 1, segs):
            lower[i, k] = (real[i, k] * inv, imag[i, k] * inv)
        yield 8 + 2 * (segs - k)
        for i in range(k + 1, segs):
            lr, li = lower[i, k]
            for j in range(k + 1, i):
                gr, gi = real[j, k], imag[j, k]
                real[i, j] = real[i, j] - (lr * gr + li * gi)
                imag[i, j] = imag[i, j] - (li * gr - lr * gi)
            real[i, i] = real[i, i] - (lr * real[i, k] + li * imag[i, k])
            br, bi = right[k]
            cr, ci = right[i]
            right[i] = (cr - (lr * br - li * bi), ci - (lr * bi + li * br))
            yield 8 * (i - k - 1) + 12
    for k in range(segs - 1, -1, -1):
        br, bi = right[k]
        vr, vi = br * inverse[k], bi * inverse[k]
        for i in range(k + 1, segs):
            lr, li = lower[i, k]
            wr, wi = found[i]
            vr = vr - (lr * wr + li * wi)
            vi = vi - (lr * wi - li * wr)
        found[k] = (vr, vi)
        yield 2 + 8 * (segs - 1 - k)


def solve_kernel(shifts, own_ref, other_ref, early_ref, late_ref, out_hbm, wide_ref, slot_ref, sem):
    half = LANES // 2
    groups, rows, _ = own_ref.shape
    chans = LANES // 2
    early, late = early_ref.shape[1], late_ref.shape[1]
    segs = 2 * rows // (2 * SUB)
    steps, pair = slot_ref.shape[:2]
    blocks = [(early_ref, at) for at in range(0, early, 256)] + [(late_ref, at) for at in range(0, late, 256)]
    sources = [lax.axis_index("bin") ^ shift for shift in shifts]
    first_half = lax.axis_index("grp") == 0
    row_bin = lax.broadcasted_iota(jnp.int32, (2 * SUB, 2 * LANES), 0) % SUB

    def copy_out(step, group):
        return pltpu.make_async_copy(
            slot_ref.at[step], out_hbm.at[pl.ds(group * SUB + step * pair, pair)], sem.at[step]
        )

    def solve(group, into):
        own = own_ref[group].astype(jnp.float32)
        other = other_ref[group].astype(jnp.float32)
        low = jnp.where(first_half, own, other)
        high = jnp.where(first_half, other, own)
        left = lax.broadcasted_iota(jnp.int32, low.shape, 1) < half
        even = jnp.where(left, low, pltpu.roll(high, half, 1))
        odd = jnp.where(left, pltpu.roll(low, half, 1), high)
        refs = []
        for seg in range(segs):
            source = odd if seg % 2 else even
            at = seg // 2 * 2 * SUB
            refs.append((source[at : at + SUB], source[at + SUB : at + 2 * SUB]))
        yield 100
        found = [None] * segs
        yield from solve_steps(refs, segs, LANES, found)
        for seg in range(segs):
            vr, vi = found[seg]
            at = (seg % 2) * LANES + seg // 2 * 2 * SUB
            here = pl.ds(at, 2 * SUB)
            wide_ref[into, here, 0:LANES] = jnp.concatenate([vr, -vi], axis=0).astype(jnp.bfloat16)
            wide_ref[into, here, LANES : 2 * LANES] = jnp.concatenate([vi, vr], axis=0).astype(
                jnp.bfloat16
            )

    solve_cost = 100 + 6 * 136 + 32 + 8 * 16 + 240 + 8 * 560 + 12 * 120 + 32 + 960

    def apply(group, beside):
        done = 0
        for step in range(steps):
            if isinstance(group, int):
                copy_out(step, group).wait()
            else:

                @pl.when(group > 0)
                def _():
                    copy_out(step, group).wait()

            tiles = wide_ref[group % 2].reshape(-1, 2 * SUB, 2 * LANES)
            weights = jnp.concatenate(
                [
                    jnp.where(
                        (row_bin == step * pair + k)[None], tiles, jnp.zeros_like(tiles)
                    ).reshape(wide_ref.shape[1:])
                    for k in range(pair)
                ],
                axis=1,
            )
            for block, (turned_ref, first) in enumerate(blocks):
                product = jnp.dot(
                    turned_ref[group, pl.ds(first, 256), :], weights, preferred_element_type=jnp.float32
                ).astype(jnp.bfloat16)
                for at in range(0, 256, chans):
                    source = sources[(block * 256 + at) // chans]
                    here = pl.ds(pl.multiple_of(source * chans, chans), chans)
                    for k in range(pair):
                        slot_ref[step, k, here, :] = product[
                            at : at + chans, k * 2 * LANES : (k + 1) * 2 * LANES
                        ]
                limit = solve_cost * (step * len(blocks) + block + 1) / (steps * len(blocks))
                while done < limit:
                    cost = next(beside, None)
                    if cost is None:
                        break
                    done += cost
            copy_out(step, group).start()
        for _ in beside:
            pass

    for _ in solve(0, 0):
        pass

    @pl.loop(0, groups - 1)
    def _(group):
        apply(group, solve(group + 1, (group + 1) % 2))

    apply(groups - 1, iter(()))
    for step in range(steps):
        copy_out(step, groups - 1).wait()


def solve_and_apply(shifts, own, other, early, late):
    groups, _, depth = early.shape
    chans = early.shape[1] + late.shape[1]
    pair = 2
    steps = SUB // pair
    return pl.pallas_call(
        functools.partial(solve_kernel, shifts),
        out_shape=jax.ShapeDtypeStruct((groups * SUB, chans, 2 * LANES), jnp.bfloat16),
        in_specs=[pl.BlockSpec(memory_space=pltpu.VMEM)] * 4,
        out_specs=pl.BlockSpec(memory_space=pltpu.HBM),
        scratch_shapes=[
            pltpu.VMEM((2, depth, 2 * LANES), jnp.bfloat16),
            pltpu.VMEM((steps, pair, chans, 2 * LANES), jnp.bfloat16),
            pltpu.SemaphoreType.DMA((steps,)),
        ],
        compiler_params=pltpu.CompilerParams(vmem_limit_bytes=VMEM_LIMIT),
        cost_estimate=pl.CostEstimate(
            flops=2 * groups * SUB * chans * depth * 2 * LANES,
            bytes_accessed=groups * SUB * chans * 4 * LANES,
            transcendentals=0,
        ),
        name="solve_apply",
    )(own, other, early, late)


def local_kernels(record, ref_index, offsets):
    chan_rows = record[0]
    devices = lax.axis_size("bin")
    groups = NB // devices // SUB
    table = host_table(L, NB).reshape(2, devices, groups, SUB, L).transpose(1, 2, 0, 3, 4)
    table = jnp.asarray(table.reshape(devices, -1, L))
    index = jnp.concatenate([ref_index, ref_index], axis=1)
    me = lambda: lax.axis_index("bin")
    got = {}
    for part in (SHIFTS[:FIRST], SHIFTS[FIRST:] + (0,)):
        made = spectra_of(
            chan_rows, offsets, table, lambda k, part=part: me() ^ part[k], len(part), True
        )
        chan_rows, *made = lax.optimization_barrier((chan_rows, *made))
        for shift, block in zip(part, made):
            pairs = [(i, i ^ shift) for i in range(devices)]
            got[shift] = lax.ppermute(block, "bin", pairs) if shift else block
    early, late = (0,) + SHIFTS[:-LATE], SHIFTS[-LATE:]
    got_early, got_late = [got[shift] for shift in early], [got[shift] for shift in late]
    own = pick_refs(index, late, got_late, pick_refs(index, early, got_early, None))
    other = lax.ppermute(own, "grp", [(0, 1), (1, 0)])
    return solve_and_apply(early + late, own, other, turn(got_early), turn(got_late))


def transform(chan_rows, starts, dft_table, bin_devices):
    seg_len = dft_table.shape[0]
    pieces = jax.vmap(lambda start_at: lax.dynamic_slice_in_dim(chan_rows, start_at, seg_len, 1))(
        starts
    )
    spectra = jnp.einsum(
        "scn,nk->ksc", pieces, dft_table, preferred_element_type=jnp.float32
    ).astype(jnp.bfloat16)
    bin_total = dft_table.shape[1] // 2
    return spectra.reshape(
        2, bin_devices, bin_total // bin_devices, starts.shape[0], chan_rows.shape[0]
    )


def local(record, ref_index, offsets):
    chan_rows = record[0]
    dft_table = make_table(L, NB)
    bin_devices = lax.axis_size("bin")
    spectra = transform(chan_rows, offsets, dft_table, bin_devices)
    channels = lax.all_to_all(spectra, "bin", split_axis=1, concat_axis=4, tiled=True)[:, 0]
    local_refs = jnp.take(channels, ref_index[0], axis=3)
    references = lax.all_gather(local_refs, "grp", axis=3, tiled=True)
    ref_real = references[0]
    ref_imag = references[1]
    ref_blocks = jnp.stack(
        [
            jnp.concatenate([ref_real, -ref_imag], axis=-1),
            jnp.concatenate([ref_imag, ref_real], axis=-1),
        ]
    )
    bins_here = channels.shape[1]
    group_size = math.gcd(bins_here, 4)
    group_count = bins_here // group_size
    real_order = ref_blocks.shape[-1]

    def solve_bins(group_index):
        first_bin = group_index * group_size
        ref_group = lax.dynamic_slice_in_dim(ref_blocks, first_bin, group_size, 1)
        chan_group = lax.dynamic_slice_in_dim(channels, first_bin, group_size, 1)
        ref_rows = jnp.swapaxes(ref_group, 0, 1).reshape(group_size, -1, real_order)
        chan_cols = jnp.swapaxes(chan_group, 0, 1).reshape(group_size, -1, chan_group.shape[-1])
        gram_small = jnp.einsum(
            "fkr,fjr->fkj", ref_rows, ref_rows, preferred_element_type=jnp.float32
        )
        small_order = gram_small.shape[-1]
        ridge_term = ridge_weight * jnp.trace(gram_small, axis1=1, axis2=2) / real_order
        factor = jnp.linalg.cholesky(
            gram_small + ridge_term[:, None, None] * jnp.eye(small_order, dtype=jnp.float32)
        )
        solved = jax.scipy.linalg.cho_solve((factor, True), chan_cols.astype(jnp.float32))
        solved_high = solved.astype(jnp.bfloat16)
        solved_low = (solved - solved_high.astype(jnp.float32)).astype(jnp.bfloat16)
        transfer_t = jnp.einsum(
            "fkr,fkc->frc", ref_rows, solved_high, preferred_element_type=jnp.float32
        )
        transfer_t = transfer_t + jnp.einsum(
            "fkr,fkc->frc", ref_rows, solved_low, preferred_element_type=jnp.float32
        )
        return jnp.swapaxes(transfer_t, 1, 2).astype(jnp.bfloat16)

    results = lax.map(solve_bins, jnp.arange(group_count))
    return results.reshape(bins_here, results.shape[2], results.shape[3])


def solution(mesh):
    placed = (P("grp", "bin", None), P("grp", None), P())
    devices, groups = mesh.shape["bin"], mesh.shape["grp"]

    def whole(record, ref_index, offsets):
        chans = record.shape[1] // devices
        kernels = (
            devices == 1 + len(SHIFTS)
            and groups == 2
            and 2 * chans == LANES
            and groups * ref_index.shape[1] == LANES
            and offsets.shape[0] == 2 * SUB
            and NB // devices % SUB == 0
            and NB // devices >= 2 * SUB
        )
        return jax.shard_map(
            local_kernels if kernels else local,
            mesh=mesh,
            in_specs=placed,
            out_specs=P("bin", "grp", None),
            check_vma=False,
        )(record, ref_index, offsets)

    return whole
```
